32 devices in a mesh: groups: 2 (over y), elem: 4 (over z), sub: 2 (over x), col: 2 (over core).
Axes of the slice: x: 2, y: 2, z: 4, core: 2. Of those that a mesh axis runs over, the one named last changes fastest.
Arguments:
- jacobian: bfloat16 [1536, 20480], P(('groups', 'elem', 'sub')), parts along dimension 0, may hold values from -0.75 to 0.75
- prolong: bfloat16 [64, 98304], P('col', ('groups', 'elem', 'sub')), parts along dimension 1, may hold values from -5 to 5
- face_pattern: int32 [1536, 4], P(('groups', 'elem', 'sub')), parts along dimension 0, may hold values from -1 to 767, as said below
- owner: int32 [1536, 1], P(('groups', 'elem', 'sub')), parts along dimension 0, may hold values from 0 to 7; in each aligned block of 96 rows (0 to 95, 96 to 191, ...) at most 24 rows name the same one
- member: int32 [1536], P(('groups', 'elem', 'sub')), parts along dimension 0, may hold values from 0 to 11
- coarse_slot: int32 [1536, 5], P(('groups', 'elem', 'sub')), parts along dimension 0, may hold values from 0 to 8
Outputs:
- coarse: float32 [64, 192, 576], P('col', ('groups', 'elem', 'sub')), parts along dimension 1
The draws below stay inside these ranges and needn't reach their ends.
There are 2 independent parts, one for each index of `groups`. The reference program is written for one: setup_inputs(seed, part) draws one part's arguments, and reference() takes and returns one part's arrays. A program takes and returns all parts, laid end to end along the dimension named above; each array names one. Nothing has to cross between parts.
Inputs may be any that keep to these rules, and one draw needn't show every extreme that they name: `face_pattern`: face 0 of each of the first 24 elements of a device names one of the last 24 elements of the previous device (-1 on the first device); face 1 of each of the last 24 names one of the first 24 elements of the next device (-1 on the last); every other face names another element of the same device. Among the 96 elements of one device, at most 24 name the same owner.
All inputs are finite; a program needn't handle non-finite values.
Results may differ from the reference program's by a relative error of at most 0.0029.
Values may be sent and summed in bfloat16 or wider, within the bound.
No kernel may reach another device: no remote copies, remote signals or barrier semaphores. Data moves between devices by JAX's collectives and lax.ppermute only.
A program may use at most 128 MiB of HBM per device.

```python
import math
import jax
import jax.numpy as jnp
import numpy as np
from jax import lax

B = 64
CB = 64
FACES = 4
CS = 9
E_DEV = 96
BND = 24
AGG_DEV = 12
CAP = 24
ELEMS = 768
AGGS = 96
N_ELEM = 4
N_SUB = 2


def draw_face_pattern(key, part):
    key = jax.random.fold_in(key, 11)
    first_key, second_key = jax.random.split(key, 2)
    glob = jnp.arange(ELEMS, dtype=jnp.int32)
    local = glob % E_DEV
    device = glob // E_DEV
    last_device = ELEMS // E_DEV - 1
    offset = jax.random.randint(first_key, (ELEMS, FACES), 1, E_DEV, dtype=jnp.int32)
    inner = device[:, None] * E_DEV + (local[:, None] + offset) % E_DEV
    picked = jax.random.randint(second_key, (ELEMS, 2), 0, BND, dtype=jnp.int32)
    lower = jnp.where(device == 0, -1, device * E_DEV - BND + picked[:, 0])
    upper = jnp.where(device == last_device, -1, (device + 1) * E_DEV + picked[:, 1])
    face_lower = jnp.where(local < BND, lower, inner[:, 0])
    face_upper = jnp.where(local >= E_DEV - BND, upper, inner[:, 1])
    return jnp.stack([face_lower, face_upper, inner[:, 2], inner[:, 3]], axis=1).astype(jnp.int32)


def plant(drawn, stream_key, least, largest):
    shape = drawn.shape
    index_at = [jax.random.randint(jax.random.fold_in(stream_key, axis), (), 0, shape[axis]) for axis in range(len(shape))]
    drawn = drawn.at[tuple(index_at)].set(least)
    longest = shape.index(max(shape))
    index_at[longest] = (index_at[longest] + 1) % shape[longest]
    return drawn.at[tuple(index_at)].set(largest)


def block_scale(own_key, shape, shards, smallest, largest):
    gain, own = 1.0, jax.random.fold_in(own_key, 6)
    for axis_at, parts in shards:
        heights = jnp.exp(jax.random.uniform(jax.random.fold_in(own, axis_at), (parts,), jnp.float32, smallest / len(shards), largest / len(shards)))
        gain = gain * jnp.repeat(heights, shape[axis_at] // parts).reshape([-1 if axis == axis_at else 1 for axis in range(len(shape))])
    return gain


def deal_out(stream_key, own, number, rows, number_of, top, limit, skew):
    ranking = jax.random.permutation(stream_key, number_of)
    heavy_load, usual = portions_of(number_of, rows * top, limit, skew, True), portions_of(number_of, rows * top, limit, skew, False)
    places = jnp.arange(number_of)

    def named(tallies, offset_by):
        used = int((tallies > 0).sum())
        fixed = max(1, used // 4)
        moved = fixed + (places - fixed + offset_by * (used - fixed)) % max(1, number_of - fixed)
        return jnp.zeros((number_of,), jnp.int32).at[ranking[jnp.where(places < fixed, places, moved)]].set(jnp.asarray(tallies, jnp.int32))

    tallies = jnp.where(number % 4 == 0, named(heavy_load, number // 4), named(usual, number - number // 4 - 1))
    mixed = jax.random.permutation(jax.random.fold_in(own, 3), number_of)
    source_of, receiver = mixed[0:number_of // 2 * 2:2], mixed[1:number_of // 2 * 2:2]
    margin = jnp.minimum(tallies[source_of] - 1, limit - tallies[receiver]) // 2
    margin = jnp.where((source_of == ranking[0]) | (receiver == ranking[0]) | (tallies[receiver] == 0), 0, jnp.maximum(margin, 0))
    moved = jax.random.randint(jax.random.fold_in(own, 4), (number_of // 2,), 0, 1 << 20) % (margin + 1)
    tallies = tallies.at[source_of].add(-moved).at[receiver].add(moved)
    items = jnp.searchsorted(jnp.cumsum(tallies), jnp.arange(rows * top), side="right").astype(jnp.int32)
    table = items.reshape(top, rows).T
    table = table[jax.random.permutation(jax.random.fold_in(own, 1), rows)]
    offset_by = jax.random.randint(jax.random.fold_in(own, 2), (rows, 1), 0, top)
    return jnp.take_along_axis(table, (jnp.arange(top)[None, :] + offset_by) % top, axis=1)


def portions_of(count, total, bound, skew, full):
    weights = [(1 << 20) // math.isqrt(grade ** skew) + 1 for grade in range(1, count + 1)]
    largest = bound if full else min(bound, max(-(-total // count), total * weights[0] // sum(weights)))
    least = 1 if total - largest >= count - 1 else 0
    holding, surplus = [largest] + [least] * (count - 1), total - largest - least * (count - 1)
    while surplus > 0:
        candidates = [i for i in range(1, count) if holding[i] < largest] or [i for i in range(1, count) if holding[i] < bound]
        whole, remaining = sum([weights[i] for i in candidates]), surplus
        for i in candidates:
            extra = min(bound - holding[i], max(1, remaining * weights[i] // whole), surplus)
            holding[i] = holding[i] + extra
            surplus = surplus - extra
    return np.array(holding)


def noise(rng, dims, scale, bound, shards=(), kind=jnp.bfloat16):
    array = scale * jax.random.normal(rng, dims, jnp.float32)
    if shards:
        array = array * block_scale(rng, dims, shards, -0.22, 0.18)
    return jnp.clip(array, -bound, bound).astype(kind)


def setup_inputs(seed: int = 0, part: int = 0) -> dict:
    key_list = jax.random.split(jax.random.key(seed), 7)
    part_splits = jax.random.split(jax.random.fold_in(key_list[6], part), 7)
    jacobian = noise(part_splits[0], (ELEMS, (FACES + 1) * B * B), B ** -0.5, 0.75, ((0, 8),))
    prolong = noise(part_splits[1], (CB, ELEMS * B), 0.35, 5.0, ((0, 2), (1, 8)))
    face_pattern = draw_face_pattern(jax.random.fold_in(jax.random.fold_in(key_list[6], part), 71), part)
    owner_keys = jax.random.split(jax.random.fold_in(part_splits[3], 1), ELEMS // E_DEV)
    owner_turns = jax.random.permutation(jax.random.fold_in(part_splits[3], 3), ELEMS // E_DEV)
    owner = jax.vmap(lambda own, number: deal_out(jax.random.fold_in(part_splits[3], 2), own, number, E_DEV, N_ELEM * N_SUB, 1, CAP, 2))(owner_keys, owner_turns).reshape((ELEMS, 1))
    member = plant(jax.random.randint(part_splits[4], (ELEMS,), 0, AGG_DEV), jax.random.fold_in(part_splits[4], 1), 0, AGG_DEV - 1).astype(jnp.int32)
    coarse_slot = plant(jax.random.randint(part_splits[5], (ELEMS, FACES + 1), 0, CS), jax.random.fold_in(part_splits[5], 1), 0, CS - 1).astype(jnp.int32)
    return dict(jacobian=jacobian, prolong=prolong, face_pattern=face_pattern, owner=owner, member=member, coarse_slot=coarse_slot)


def reference(jacobian, prolong, face_pattern, owner, member, coarse_slot):
    blocks_p = prolong.reshape(CB, ELEMS, B).transpose(1, 2, 0)
    blocks_a = jacobian.reshape(ELEMS, FACES + 1, B, B)
    selfcol = jnp.arange(ELEMS, dtype=jnp.int32)[:, None]
    columns = jnp.concatenate([selfcol, face_pattern.astype(jnp.int32)], axis=1)
    present = columns >= 0
    safe = jnp.where(present, columns, 0).astype(jnp.int32)
    target = ((owner[:, 0] * AGG_DEV + member)[:, None] * CS + coarse_slot).astype(jnp.int32)
    count = ELEMS // E_DEV

    def one_block(carry, index):
        start = (index * E_DEV).astype(jnp.int32)
        part_a = lax.dynamic_slice_in_dim(blocks_a, start, E_DEV, 0)
        part_idx = lax.dynamic_slice_in_dim(safe, start, E_DEV, 0)
        part_present = lax.dynamic_slice_in_dim(present, start, E_DEV, 0)
        part_own = lax.dynamic_slice_in_dim(blocks_p, start, E_DEV, 0)
        part_target = lax.dynamic_slice_in_dim(target, start, E_DEV, 0)
        neighbour_rows = blocks_p[part_idx] * part_present[:, :, None, None].astype(blocks_p.dtype)
        product = jnp.einsum("ejik,ejkc->ejic", part_a.astype(jnp.float32),
                             neighbour_rows.astype(jnp.float32)).astype(jnp.bfloat16)
        contribution = jnp.einsum("eir,ejic->ejrc", part_own.astype(jnp.float32),
                                  product.astype(jnp.float32))
        carry = carry.at[part_target.reshape(-1)].add(contribution.reshape(-1, CB, CB))
        return carry, None

    start_sum = jnp.zeros((AGGS * CS, CB, CB), jnp.float32)
    total, unused = lax.scan(one_block, start_sum, jnp.arange(count, dtype=jnp.int32))
    coarse = total.reshape(AGGS, CS, CB, CB).transpose(3, 0, 1, 2).reshape(CB, AGGS, CS * CB)
    return coarse
```

```python
import functools

import jax
import jax.numpy as jnp
from jax import lax
from jax.experimental import pallas as pl
from jax.experimental.pallas import tpu as pltpu
from jax.sharding import PartitionSpec as P

B = 64
CB = 64
FACES = 4
CS = 9
AGG_DEV = 12
BLOCKS = AGG_DEV * CS
PAIRS = BLOCKS // 2
STEP = 16
UNROLL = 4
VMEM = pl.BlockSpec(memory_space=pltpu.VMEM)
SMEM = pl.BlockSpec(memory_space=pltpu.SMEM)
NT = (((1,), (1,)), ((), ()))


def params(mib=48):
    return pltpu.CompilerParams(vmem_limit_bytes=mib * 1024 * 1024)


def halo(cells, width):
    axes = ("elem", "sub")
    count = lax.axis_size(axes)
    up = [(i, i + 1) for i in range(count - 1)]
    down = [(i + 1, i) for i in range(count - 1)]
    return (
        lax.ppermute(cells[:, -width:], axes, up),
        lax.ppermute(cells[:, :width], axes, down),
    )


def chunk_order(count):
    table = []
    for z in range(count):
        table.append(sorted(range(count), key=lambda d: (-abs(d - z), (d < z) == (2 * z < count))))
    return table


def lists_kernel(elems, owner_ref, member_ref, slot_ref, table_ref, list_ref, count_ref, target_ref):
    me = lax.axis_index("sub")
    z = lax.axis_index("elem")
    room = list_ref.shape[1]

    def fill(i, c):
        list_ref[0, i] = elems
        list_ref[1, i] = elems
        return c

    lax.fori_loop(0, room, fill, 0)

    def place(e, counts):
        other, own = counts
        owner = owner_ref[e]
        side = jnp.where(owner % 2 == me, 1, 0)
        list_ref[side, jnp.where(side == 1, own, other)] = e
        base = table_ref[z, owner // 2] * BLOCKS + member_ref[e] * CS
        for j in range(FACES + 1):
            target_ref[j, e] = base + slot_ref[j, e]
        return other + 1 - side, own + side

    other, own = lax.fori_loop(0, elems, place, (0, 0))
    count_ref[0] = other
    count_ref[1] = own


def prep_kernel(elems, owner_ref, member_ref, slot_ref, table_ref, jac_ref,
                rows_ref, list_ref, count_ref, target_ref, wide):
    @pl.when(pl.program_id(0) == 0)
    def _():
        lists_kernel(elems, owner_ref, member_ref, slot_ref, table_ref, list_ref, count_ref, target_ref)

    tiles = jac_ref.shape[1] // 128
    for t in range(tiles):
        wide[t * STEP:(t + 1) * STEP, :] = jac_ref[:, t * 128:(t + 1) * 128].astype(jnp.float32)
    for e in range(STEP):
        rows_ref[e] = wide[pl.ds(e, tiles, stride=STEP), :].astype(jnp.bfloat16)


def accumulate(which, elems, trash, list_ref, count_ref, target_ref, face_ref, first_row,
               rows_ref, near_ref, weight_ref, total):
    low = lax.broadcasted_iota(jnp.int32, (32, 128), 1) < B
    high = jnp.where(low, 0, 1)
    absent = near_ref.shape[0] - 1

    def body(it, carry):
        for u in range(UNROLL):
            raw = list_ref[which, it * UNROLL + u]
            e = jnp.minimum(raw, elems - 1)
            valid = raw < elems
            products = []
            for j in range(FACES + 1):
                if j == 0:
                    at = e + elems // 4
                else:
                    face = face_ref[j - 1, e]
                    at = jnp.where(face >= 0, face - first_row, absent)
                block = rows_ref[e, j * 32:(j + 1) * 32, :]
                zero = jnp.zeros_like(block)
                weights = jnp.concatenate([jnp.where(low, block, zero), jnp.where(low, zero, block)], axis=0)
                products.append(lax.dot_general(near_ref[at], weights, NT, preferred_element_type=jnp.float32))
            product = jnp.concatenate(products, axis=0).astype(jnp.bfloat16)
            own = weight_ref[e]
            own = jnp.concatenate([own, own], axis=0)
            result = lax.dot_general(product, own, NT, preferred_element_type=jnp.float32)
            for j in range(FACES + 1):
                target = jnp.where(valid, target_ref[j, e], 2 * trash)
                pair = target // 2
                half = target % 2
                part = result[j * 32:(j + 1) * 32, :]
                total[pair] += jnp.where(high == half, part, 0.0)
        return carry

    steps = (count_ref[which] + UNROLL - 1) // UNROLL
    lax.fori_loop(0, steps, body, 0)


def near_blocks(near_ref, base, cells_ref):
    low = lax.broadcasted_iota(jnp.int32, (32, 128), 1) < B
    for p in range(cells_ref.shape[1] // 128):
        pair = cells_ref[:, p * 128:(p + 1) * 128].astype(jnp.float32)
        turned = pltpu.roll(pair, B, 1)
        near_ref[base + 2 * p] = jnp.where(low, pair, turned).astype(jnp.bfloat16)
        near_ref[base + 2 * p + 1] = jnp.where(low, turned, pair).astype(jnp.bfloat16)


def own_weights(weight_ref, side, cells_ref):
    row = lax.broadcasted_iota(jnp.int32, (128, B), 0)
    col = lax.broadcasted_iota(jnp.int32, (128, B), 1)
    source = 2 * (col % 32) + col // 32
    picks = [jnp.where(row == source + h * B, 1.0, 0.0).astype(jnp.bfloat16) for h in range(2)]
    at = pl.ds(pl.multiple_of(side * 32, 32), 32)
    for p in range(cells_ref.shape[1] // 128):
        pair = cells_ref[:, p * 128:(p + 1) * 128]
        for h in range(2):
            moved = jnp.dot(pair, picks[h], preferred_element_type=jnp.float32)
            weight_ref[2 * p + h, at, :] = moved.astype(jnp.bfloat16)


def first_kernel(elems, list_ref, count_ref, target_ref, face_ref, rows_ref, cells_ref, before_ref, after_ref,
                 other_ref, *rest):
    outs, (near_ref, weight_ref, total) = rest[:-3], rest[-3:]
    rim = elems // 4
    col = lax.axis_index("col")
    near_blocks(near_ref, 0, before_ref)
    near_blocks(near_ref, rim, cells_ref)
    near_blocks(near_ref, rim + elems, after_ref)
    near_ref[near_ref.shape[0] - 1] = jnp.zeros((32, 128), jnp.bfloat16)
    own_weights(weight_ref, col, cells_ref)
    own_weights(weight_ref, 1 - col, other_ref)
    total[...] = jnp.zeros_like(total)
    device = lax.axis_index("elem") * lax.axis_size("sub") + lax.axis_index("sub")
    first_row = device * elems - rim
    accumulate(0, elems, total.shape[0] - 1, list_ref, count_ref, target_ref, face_ref, first_row,
               rows_ref, near_ref, weight_ref, total)
    for k, out in enumerate(outs):
        out[...] = total[k * PAIRS:(k + 1) * PAIRS].astype(jnp.bfloat16)


def second_kernel(elems, list_ref, count_ref, target_ref, face_ref, rows_ref, near_ref, weight_ref, *rest):
    outs, total = rest[:-1], rest[-1]
    rim = elems // 4
    total[...] = jnp.zeros_like(total)
    device = lax.axis_index("elem") * lax.axis_size("sub") + lax.axis_index("sub")
    first_row = device * elems - rim
    accumulate(1, elems, total.shape[0] - 1, list_ref, count_ref, target_ref, face_ref, first_row,
               rows_ref, near_ref, weight_ref, total)
    for k, out in enumerate(outs):
        out[...] = total[k * PAIRS:(k + 1) * PAIRS]


def last_kernel(own_ref, across_ref, up_ref, down_ref, out_ref, total):
    total[...] = (own_ref[...] + across_ref[...].astype(jnp.float32)
                  + up_ref[...].astype(jnp.float32) + down_ref[...].astype(jnp.float32))
    low = lax.broadcasted_iota(jnp.int32, (32, 128), 1) < B
    for a in range(AGG_DEV):
        first = a * CS // 2
        for q in range(CS // 2):
            if a % 2 == 0:
                out_ref[a, :, q * 128:(q + 1) * 128] = total[first + q]
            else:
                out_ref[a, :, q * 128:(q + 1) * 128] = jnp.where(
                    low, pltpu.roll(total[first + q], B, 1), pltpu.roll(total[first + q + 1], B, 1))
        last = total[first + CS // 2]
        if a % 2 == 1:
            last = pltpu.roll(last, B, 1)
        out_ref[a, :, (CS // 2) * 128:] = last[:, :B]


def dense(jacobian, prolong, face_pattern, owner, member, coarse_slot):
    elems = jacobian.shape[0]
    half = prolong.shape[0]
    count = lax.axis_size("elem")
    z = lax.axis_index("elem")
    rim = elems // 4
    tiles = jacobian.shape[1] // 128
    order = chunk_order(count)
    position = [[order[y].index(d) for d in range(count)] for y in range(count)]

    before, after = halo(prolong, rim * B)
    other = lax.ppermute(prolong, "col", [(0, 1), (1, 0)])

    room = elems + 2 * UNROLL
    rows, lists, counts, targets = pl.pallas_call(
        functools.partial(prep_kernel, elems),
        grid=(elems // STEP,),
        in_specs=[SMEM, SMEM, SMEM, SMEM, pl.BlockSpec((STEP, jacobian.shape[1]), lambda i: (i, 0))],
        out_specs=[pl.BlockSpec((STEP, tiles, 128), lambda i: (i, 0, 0)), SMEM, SMEM, SMEM],
        out_shape=[
            jax.ShapeDtypeStruct((elems, tiles, 128), jnp.bfloat16),
            jax.ShapeDtypeStruct((2, room), jnp.int32),
            jax.ShapeDtypeStruct((2,), jnp.int32),
            jax.ShapeDtypeStruct((FACES + 1, elems), jnp.int32),
        ],
        scratch_shapes=[pltpu.VMEM((tiles * STEP, 128), jnp.float32)],
        compiler_params=params(),
        cost_estimate=pl.CostEstimate(flops=0, bytes_accessed=2 * jacobian.size * 2, transcendentals=0),
        name="prep",
    )(owner.reshape(elems), member, coarse_slot.T, jnp.asarray(position, jnp.int32), jacobian)
    faces = face_pattern.T

    table = (count * PAIRS + 1, half, 2 * B)
    flops = elems * (FACES + 1) * B * B * half * 2
    results = pl.pallas_call(
        functools.partial(first_kernel, elems),
        in_specs=[SMEM] * 4 + [VMEM] * 5,
        out_specs=[VMEM] * (count + 2),
        out_shape=[jax.ShapeDtypeStruct((PAIRS, half, 2 * B), jnp.bfloat16)] * count + [
            jax.ShapeDtypeStruct((elems + 2 * rim + 1, half, 2 * B), jnp.bfloat16),
            jax.ShapeDtypeStruct((elems, CB, B), jnp.bfloat16),
        ],
        scratch_shapes=[pltpu.VMEM(table, jnp.float32)],
        compiler_params=params(),
        cost_estimate=pl.CostEstimate(flops=flops, bytes_accessed=8 << 20, transcendentals=0),
        name="first",
    )(lists, counts, targets, faces, rows, prolong, before, after, other)
    sent, (near, weights) = results[:count], results[count:]
    arrived = [lax.ppermute(block, "sub", [(0, 1), (1, 0)]) for block in sent]
    kept = pl.pallas_call(
        functools.partial(second_kernel, elems),
        in_specs=[SMEM] * 4 + [VMEM] * 3,
        out_specs=[VMEM] * count,
        out_shape=[jax.ShapeDtypeStruct((PAIRS, half, 2 * B), jnp.float32)] * count,
        scratch_shapes=[pltpu.VMEM(table, jnp.float32)],
        compiler_params=params(),
        cost_estimate=pl.CostEstimate(flops=flops, bytes_accessed=8 << 20, transcendentals=0),
        name="second",
    )(lists, counts, targets, faces, rows, near, weights)

    def chosen(step, up):
        groups = {}
        for y in range(count):
            d = y + count - step if up else y - count + step
            if 0 <= d < count:
                groups.setdefault(position[y][d], []).append(y)
        value = None
        for k, places in groups.items():
            block = kept[k] + arrived[k].astype(jnp.float32)
            if value is None:
                value = block
            else:
                here = functools.reduce(jnp.logical_or, [z == y for y in places])
                value = jnp.where(here, block, value)
        return value

    up = down = None
    for step in range(1, count):
        rise, fall = chosen(step, True), chosen(step, False)
        if up is not None:
            rise, fall = rise + up.astype(jnp.float32), fall + down.astype(jnp.float32)
        ends = min(step, count - 1)
        up = lax.ppermute(rise.astype(jnp.bfloat16), "elem", [(y, y + 1) for y in range(ends)])
        down = lax.ppermute(fall.astype(jnp.bfloat16), "elem", [(count - 1 - y, count - 2 - y) for y in range(ends)])

    coarse = pl.pallas_call(
        last_kernel,
        in_specs=[VMEM] * 4,
        out_specs=VMEM,
        out_shape=jax.ShapeDtypeStruct((AGG_DEV, half, CS * CB), jnp.float32),
        scratch_shapes=[pltpu.VMEM((PAIRS, half, 2 * B), jnp.float32)],
        compiler_params=params(),
        name="last",
    )(kept[count - 1], arrived[count - 1], up, down)
    return coarse.transpose(1, 0, 2)


def direct(jacobian, prolong, face_pattern, owner, member, coarse_slot):
    elems = jacobian.shape[0]
    owners = lax.axis_size(("elem", "sub"))
    capacity = max(2, 2 * elems // owners)
    device = lax.axis_index(("elem", "sub"))
    half = prolong.shape[0]
    rim = elems // 4
    before, after = halo(prolong, rim * B)
    ghosts = jnp.concatenate([before, prolong, after], axis=1).reshape(half, elems + 2 * rim, B)
    whole = lax.all_gather(prolong, "col", axis=0, tiled=True).reshape(CB, elems, B)
    first_row = device * elems - rim
    selfcol = jnp.arange(elems, dtype=jnp.int32)[:, None] + rim
    remote = jnp.where(face_pattern >= 0, face_pattern - first_row, 0)
    columns = jnp.concatenate([selfcol, remote], axis=1)
    present = jnp.concatenate([jnp.ones((elems, 1), jnp.bool_), face_pattern >= 0], axis=1)
    neighbour_rows = ghosts[:, columns, :] * present[None, :, :, None].astype(jnp.bfloat16)
    blocks = jacobian.reshape(elems, FACES + 1, B, B)
    product = jnp.einsum(
        "ejik,cejk->ejic", blocks, neighbour_rows, preferred_element_type=jnp.float32
    ).astype(jnp.bfloat16)
    owner_flat = owner[:, 0]
    marks = (owner_flat[:, None] == jnp.arange(owners, dtype=jnp.int32)[None, :]).astype(jnp.int32)
    ranking = jnp.sum(jnp.cumsum(marks, axis=0) * marks, axis=1) - 1
    place = owner_flat * capacity + ranking
    target = member[:, None] * CS + coarse_slot
    slots = owners * capacity
    labels = jnp.full((slots, FACES + 1), -1, jnp.int32).at[place].set(target)
    contribution = jnp.einsum("rei,ejic->ejcr", whole, product, preferred_element_type=jnp.float32)
    payload = jnp.zeros((slots, FACES + 1, half, CB), jnp.float32).at[place].set(contribution)
    axes = ("elem", "sub")
    arrived = lax.all_to_all(payload, axes, split_axis=0, concat_axis=0, tiled=True)
    arrived_labels = lax.all_to_all(labels, axes, split_axis=0, concat_axis=0, tiled=True)
    items = slots * (FACES + 1)
    values = arrived.reshape(items, half * CB)
    flat_labels = arrived_labels.reshape(items)
    destination = jnp.where(flat_labels >= 0, flat_labels, BLOCKS).astype(jnp.int32)
    summed = jnp.zeros((BLOCKS, half * CB), jnp.float32).at[destination].add(values, mode="drop")
    summed = summed.reshape(AGG_DEV, CS, half, CB).transpose(2, 0, 1, 3)
    return summed.reshape(half, AGG_DEV, CS * CB)


def shards(jacobian, *rest):
    elems = jacobian.shape[0]
    owners = lax.axis_size(("elem", "sub"))
    capacity = max(2, 2 * elems // owners)
    if lax.axis_size("sub") == 2 and BLOCKS <= capacity * (FACES + 1):
        return dense(jacobian, *rest)
    return direct(jacobian, *rest)


def solution(mesh):
    in_specs = (
        P(("groups", "elem", "sub"), None),
        P("col", ("groups", "elem", "sub")),
        P(("groups", "elem", "sub"), None),
        P(("groups", "elem", "sub"), None),
        P(("groups", "elem", "sub")),
        P(("groups", "elem", "sub"), None),
    )
    out_specs = P("col", ("groups", "elem", "sub"), None)
    return jax.shard_map(shards, mesh=mesh, in_specs=in_specs, out_specs=out_specs, check_vma=False)
```

```python
import functools

import jax
import jax.numpy as jnp
from jax import lax
from jax.experimental import pallas as pl
from jax.experimental.pallas import tpu as pltpu
from jax.sharding import PartitionSpec as P

B = 64
CB = 64
FACES = 4
CS = 9
AGG_DEV = 12
BLOCKS = AGG_DEV * CS
PAIRS = BLOCKS // 2
STEP = 16
UNROLL = 4
VMEM = pl.BlockSpec(memory_space=pltpu.VMEM)
SMEM = pl.BlockSpec(memory_space=pltpu.SMEM)
NT = (((1,), (1,)), ((), ()))


def params(mib=16):
    return pltpu.CompilerParams(vmem_limit_bytes=mib * 1024 * 1024)


def halo(cells, width):
    axes = ("elem", "sub")
    count = lax.axis_size(axes)
    up = [(i, i + 1) for i in range(count - 1)]
    down = [(i + 1, i) for i in range(count - 1)]
    return (
        lax.ppermute(cells[:, -width:], axes, up),
        lax.ppermute(cells[:, :width], axes, down),
    )


MEMBER, SLOT, FACE = 1, 2, 2 + FACES + 1


def place_of(count, z, dest):
    low = 2 * z < count
    if dest == z:
        return count - 1
    if low:
        return z + count - dest - 1 if dest > z else dest
    return count - 1 - z + dest if dest < z else count - 1 - dest


def group_lists(elems, count, ints_ref, list_ref, count_ref, group_ref):
    me = lax.axis_index("sub")
    z = lax.axis_index("elem")
    for d in range(count):
        place = place_of(count, 0, d)
        for y in range(1, count):
            place = jnp.where(z == y, place_of(count, y, d), place)
        for x in range(2):
            group_ref[2 * d + x] = place + jnp.where(me == x, count, 0)
    for g in range(2 * count):
        count_ref[g] = 0

    def put(e, carry):
        group = group_ref[ints_ref[0, e]]
        at = count_ref[group]
        list_ref[group, at] = e
        count_ref[group] = at + 1
        return carry

    lax.fori_loop(0, elems, put, 0, unroll=4)


def prep_kernel(elems, count, ints_ref, jac_ref, cells_ref, other_ref,
                rows_ref, near_ref, weight_ref, list_ref, count_ref, wide, group_ref):
    @pl.when(pl.program_id(0) == 0)
    def _():
        group_lists(elems, count, ints_ref, list_ref, count_ref, group_ref)

    tiles = jac_ref.shape[1] // 128
    for t in range(tiles):
        wide[t * STEP:(t + 1) * STEP, :] = jac_ref[:, t * 128:(t + 1) * 128].astype(jnp.float32)
    near_blocks(near_ref, 0, cells_ref)
    col = lax.axis_index("col")
    own_weights(weight_ref, col, cells_ref)
    own_weights(weight_ref, 1 - col, other_ref)
    for e in range(STEP):
        rows_ref[e] = wide[pl.ds(e, tiles, stride=STEP), :].astype(jnp.bfloat16)


def accumulate(group, elems, ints_ref, list_ref, count_ref, rows_ref, near_ref, weight_ref, total):
    low = lax.broadcasted_iota(jnp.int32, (32, 128), 1) < B
    high = jnp.where(low, 0, 1)
    rim = elems // 4
    absent = near_ref.shape[0] - 1
    trash = 2 * PAIRS
    device = lax.axis_index("elem") * lax.axis_size("sub") + lax.axis_index("sub")
    first_row = device * elems - rim
    number = count_ref[group]
    total[...] = jnp.zeros_like(total)

    def body(it, carry):
        for u in range(UNROLL):
            at = it * UNROLL + u
            valid = at < number
            e = jnp.where(valid, list_ref[group, at], 0)
            products = []
            for j in range(FACES + 1):
                if j == 0:
                    cell = e + rim
                else:
                    face = ints_ref[FACE + j - 1, e]
                    cell = jnp.where(face >= 0, face - first_row, absent)
                block = rows_ref[e, j * 32:(j + 1) * 32, :]
                zero = jnp.zeros_like(block)
                weights = jnp.concatenate([jnp.where(low, block, zero), jnp.where(low, zero, block)], axis=0)
                products.append(lax.dot_general(near_ref[cell], weights, NT, preferred_element_type=jnp.float32))
            product = jnp.concatenate(products, axis=0).astype(jnp.bfloat16)
            own = weight_ref[e]
            own = jnp.concatenate([own, own], axis=0)
            result = lax.dot_general(product, own, NT, preferred_element_type=jnp.float32)
            base = ints_ref[MEMBER, e] * CS
            for j in range(FACES + 1):
                target = jnp.where(valid, base + ints_ref[SLOT + j, e], trash)
                part = result[j * 32:(j + 1) * 32, :]
                total[target // 2] += jnp.where(high == target % 2, part, 0.0)
        return carry

    lax.fori_loop(0, (number + UNROLL - 1) // UNROLL, body, 0)


def near_blocks(near_ref, base, cells_ref):
    low = lax.broadcasted_iota(jnp.int32, (32, 128), 1) < B
    for p in range(cells_ref.shape[1] // 128):
        pair = cells_ref[:, p * 128:(p + 1) * 128].astype(jnp.float32)
        turned = pltpu.roll(pair, B, 1)
        near_ref[base + 2 * p] = jnp.where(low, pair, turned).astype(jnp.bfloat16)
        near_ref[base + 2 * p + 1] = jnp.where(low, turned, pair).astype(jnp.bfloat16)


def own_weights(weight_ref, side, cells_ref):
    row = lax.broadcasted_iota(jnp.int32, (128, B), 0)
    col = lax.broadcasted_iota(jnp.int32, (128, B), 1)
    source = 2 * (col % 32) + col // 32
    picks = [jnp.where(row == source + h * B, 1.0, 0.0).astype(jnp.bfloat16) for h in range(2)]
    at = pl.ds(pl.multiple_of(side * 32, 32), 32)
    for p in range(cells_ref.shape[1] // 128):
        pair = cells_ref[:, p * 128:(p + 1) * 128]
        for h in range(2):
            moved = jnp.dot(pair, picks[h], preferred_element_type=jnp.float32)
            weight_ref[2 * p + h, at, :] = moved.astype(jnp.bfloat16)


def first_kernel(elems, ints_ref, list_ref, count_ref, rows_ref, own_ref, weight_ref, before_ref, after_ref,
                 sent_ref, near_ref, total):
    rim = elems // 4
    near_blocks(near_ref, 0, before_ref)
    near_ref[rim:rim + elems] = own_ref[...]
    near_blocks(near_ref, rim + elems, after_ref)
    near_ref[near_ref.shape[0] - 1] = jnp.zeros((32, 128), jnp.bfloat16)
    accumulate(0, elems, ints_ref, list_ref, count_ref, rows_ref, near_ref, weight_ref, total)
    sent_ref[...] = total[:PAIRS].astype(jnp.bfloat16)


def next_kernel(elems, groups, ints_ref, list_ref, count_ref, rows_ref, near_ref, weight_ref, after_ref, *rest):
    outs, total = rest[:-1], rest[-1]
    for group, out in zip(groups, outs):
        accumulate(group, elems, ints_ref, list_ref, count_ref, rows_ref, near_ref, weight_ref, total)
        out[...] = total[:PAIRS].astype(out.dtype)


def last_kernel(own_ref, across_ref, up_ref, down_ref, out_ref, total):
    total[...] = (own_ref[...] + across_ref[...].astype(jnp.float32)
                  + up_ref[...].astype(jnp.float32) + down_ref[...].astype(jnp.float32))
    low = lax.broadcasted_iota(jnp.int32, (32, 128), 1) < B
    for a in range(AGG_DEV):
        first = a * CS // 2
        for q in range(CS // 2):
            if a % 2 == 0:
                out_ref[a, :, q * 128:(q + 1) * 128] = total[first + q]
            else:
                out_ref[a, :, q * 128:(q + 1) * 128] = jnp.where(
                    low, pltpu.roll(total[first + q], B, 1), pltpu.roll(total[first + q + 1], B, 1))
        last = total[first + CS // 2]
        if a % 2 == 1:
            last = pltpu.roll(last, B, 1)
        out_ref[a, :, (CS // 2) * 128:] = last[:, :B]


def dense(jacobian, prolong, face_pattern, owner, member, coarse_slot):
    elems = jacobian.shape[0]
    half = prolong.shape[0]
    count = lax.axis_size("elem")
    z = lax.axis_index("elem")
    rim = elems // 4
    tiles = jacobian.shape[1] // 128
    capacity = 2 * elems // (2 * count)
    cost = pl.CostEstimate(flops=1000, bytes_accessed=1000, transcendentals=0)

    other = lax.ppermute(prolong, "col", [(0, 1), (1, 0)])
    before, after = halo(prolong, rim * B)
    ints = jnp.concatenate([owner.T, member[None], coarse_slot.T, face_pattern.T], axis=0)

    cells = pl.BlockSpec((half, STEP * B), lambda i: (0, i))
    rows, own_near, weights, lists, counts = pl.pallas_call(
        functools.partial(prep_kernel, elems, count),
        grid=(elems // STEP,),
        in_specs=[SMEM, pl.BlockSpec((STEP, jacobian.shape[1]), lambda i: (i, 0)), cells, cells],
        out_specs=[
            pl.BlockSpec((STEP, tiles, 128), lambda i: (i, 0, 0)),
            pl.BlockSpec((STEP, half, 2 * B), lambda i: (i, 0, 0)),
            pl.BlockSpec((STEP, CB, B), lambda i: (i, 0, 0)),
            SMEM,
            SMEM,
        ],
        out_shape=[
            jax.ShapeDtypeStruct((elems, tiles, 128), jnp.bfloat16),
            jax.ShapeDtypeStruct((elems, half, 2 * B), jnp.bfloat16),
            jax.ShapeDtypeStruct((elems, CB, B), jnp.bfloat16),
            jax.ShapeDtypeStruct((2 * count, capacity + UNROLL), jnp.int32),
            jax.ShapeDtypeStruct((2 * count,), jnp.int32),
        ],
        scratch_shapes=[pltpu.VMEM((tiles * STEP, 128), jnp.float32), pltpu.SMEM((2 * count,), jnp.int32)],
        compiler_params=params(),
        cost_estimate=cost,
        name="prep",
    )(ints, jacobian, prolong, other)

    table = (PAIRS, half, 2 * B)
    total = pltpu.VMEM((PAIRS + 1, half, 2 * B), jnp.float32)
    sent, near = pl.pallas_call(
        functools.partial(first_kernel, elems),
        in_specs=[SMEM] * 3 + [VMEM] * 5,
        out_specs=[VMEM] * 2,
        out_shape=[
            jax.ShapeDtypeStruct(table, jnp.bfloat16),
            jax.ShapeDtypeStruct((elems + 2 * rim + 1, half, 2 * B), jnp.bfloat16),
        ],
        scratch_shapes=[total],
        compiler_params=params(),
        cost_estimate=cost,
        name="first",
    )(ints, lists, counts, rows, own_near, weights, before, after)
    arrived = [lax.ppermute(sent, "sub", [(0, 1), (1, 0)])]

    kept = []
    for k in range(count):
        more = k + 1 < count
        shapes = [jax.ShapeDtypeStruct(table, jnp.bfloat16)] * more + [jax.ShapeDtypeStruct(table, jnp.float32)]
        outs = pl.pallas_call(
            functools.partial(next_kernel, elems, [k + 1] * more + [count + k]),
            in_specs=[SMEM] * 3 + [VMEM] * 3 + [pl.BlockSpec(memory_space=pl.ANY)],
            out_specs=[VMEM] * len(shapes),
            out_shape=shapes,
            scratch_shapes=[total],
            compiler_params=params(),
            cost_estimate=cost,
            name="next_%d" % k,
        )(ints, lists, counts, rows, near, weights, sent)
        kept.append(outs[-1])
        if more:
            sent = outs[0]
            arrived.append(lax.ppermute(sent, "sub", [(0, 1), (1, 0)]))

    def chosen(step, up):
        groups = {}
        for y in range(count):
            d = y + count - step if up else y - count + step
            if 0 <= d < count:
                groups.setdefault(place_of(count, y, d), []).append(y)
        value = None
        for k in sorted(groups, reverse=True):
            block = kept[k] + arrived[k].astype(jnp.float32)
            if value is None:
                value = block
            else:
                here = functools.reduce(jnp.logical_or, [z == y for y in groups[k]])
                value = jnp.where(here, block, value)
        return value

    up = down = None
    for step in range(1, count):
        rise, fall = chosen(step, True), chosen(step, False)
        if up is not None:
            rise, fall = rise + up.astype(jnp.float32), fall + down.astype(jnp.float32)
        ends = min(step, count - 1)
        up = lax.ppermute(rise.astype(jnp.bfloat16), "elem", [(y, y + 1) for y in range(ends)])
        down = lax.ppermute(fall.astype(jnp.bfloat16), "elem", [(count - 1 - y, count - 2 - y) for y in range(ends)])

    coarse = pl.pallas_call(
        last_kernel,
        in_specs=[VMEM] * 4,
        out_specs=VMEM,
        out_shape=jax.ShapeDtypeStruct((AGG_DEV, half, CS * CB), jnp.float32),
        scratch_shapes=[pltpu.VMEM(table, jnp.float32)],
        compiler_params=params(),
        cost_estimate=cost,
        name="last",
    )(kept[count - 1], arrived[count - 1], up, down)
    return coarse.transpose(1, 0, 2)


def direct(jacobian, prolong, face_pattern, owner, member, coarse_slot):
    elems = jacobian.shape[0]
    owners = lax.axis_size(("elem", "sub"))
    capacity = max(2, 2 * elems // owners)
    device = lax.axis_index(("elem", "sub"))
    half = prolong.shape[0]
    rim = elems // 4
    before, after = halo(prolong, rim * B)
    ghosts = jnp.concatenate([before, prolong, after], axis=1).reshape(half, elems + 2 * rim, B)
    whole = lax.all_gather(prolong, "col", axis=0, tiled=True).reshape(CB, elems, B)
    first_row = device * elems - rim
    selfcol = jnp.arange(elems, dtype=jnp.int32)[:, None] + rim
    remote = jnp.where(face_pattern >= 0, face_pattern - first_row, 0)
    columns = jnp.concatenate([selfcol, remote], axis=1)
    present = jnp.concatenate([jnp.ones((elems, 1), jnp.bool_), face_pattern >= 0], axis=1)
    neighbour_rows = ghosts[:, columns, :] * present[None, :, :, None].astype(jnp.bfloat16)
    blocks = jacobian.reshape(elems, FACES + 1, B, B)
    product = jnp.einsum(
        "ejik,cejk->ejic", blocks, neighbour_rows, preferred_element_type=jnp.float32
    ).astype(jnp.bfloat16)
    owner_flat = owner[:, 0]
    marks = (owner_flat[:, None] == jnp.arange(owners, dtype=jnp.int32)[None, :]).astype(jnp.int32)
    ranking = jnp.sum(jnp.cumsum(marks, axis=0) * marks, axis=1) - 1
    place = owner_flat * capacity + ranking
    target = member[:, None] * CS + coarse_slot
    slots = owners * capacity
    labels = jnp.full((slots, FACES + 1), -1, jnp.int32).at[place].set(target)
    contribution = jnp.einsum("rei,ejic->ejcr", whole, product, preferred_element_type=jnp.float32)
    payload = jnp.zeros((slots, FACES + 1, half, CB), jnp.float32).at[place].set(contribution)
    axes = ("elem", "sub")
    arrived = lax.all_to_all(payload, axes, split_axis=0, concat_axis=0, tiled=True)
    arrived_labels = lax.all_to_all(labels, axes, split_axis=0, concat_axis=0, tiled=True)
    items = slots * (FACES + 1)
    values = arrived.reshape(items, half * CB)
    flat_labels = arrived_labels.reshape(items)
    destination = jnp.where(flat_labels >= 0, flat_labels, BLOCKS).astype(jnp.int32)
    summed = jnp.zeros((BLOCKS, half * CB), jnp.float32).at[destination].add(values, mode="drop")
    summed = summed.reshape(AGG_DEV, CS, half, CB).transpose(2, 0, 1, 3)
    return summed.reshape(half, AGG_DEV, CS * CB)


def shards(jacobian, *rest):
    elems = jacobian.shape[0]
    owners = lax.axis_size(("elem", "sub"))
    capacity = max(2, 2 * elems // owners)
    if lax.axis_size("sub") == 2 and BLOCKS <= capacity * (FACES + 1):
        return dense(jacobian, *rest)
    return direct(jacobian, *rest)


def solution(mesh):
    in_specs = (
        P(("groups", "elem", "sub"), None),
        P("col", ("groups", "elem", "sub")),
        P(("groups", "elem", "sub"), None),
        P(("groups", "elem", "sub"), None),
        P(("groups", "elem", "sub")),
        P(("groups", "elem", "sub"), None),
    )
    out_specs = P("col", ("groups", "elem", "sub"), None)
    return jax.shard_map(shards, mesh=mesh, in_specs=in_specs, out_specs=out_specs, check_vma=False)
```

```python
import functools

import jax
import jax.numpy as jnp
from jax import lax
from jax.experimental import pallas as pl
from jax.experimental.pallas import tpu as pltpu
from jax.sharding import PartitionSpec as P

B = 64
CB = 64
FACES = 4
CS = 9
AGG_DEV = 12
BLOCKS = AGG_DEV * CS
PAIRS = BLOCKS // 2
STEP = 16
UNROLL = 8
VMEM = pl.BlockSpec(memory_space=pltpu.VMEM)
SMEM = pl.BlockSpec(memory_space=pltpu.SMEM)
NT = (((1,), (1,)), ((), ()))


def params(mib=16):
    return pltpu.CompilerParams(vmem_limit_bytes=mib * 1024 * 1024)


def halo(cells, width):
    axes = ("elem", "sub")
    count = lax.axis_size(axes)
    up = [(i, i + 1) for i in range(count - 1)]
    down = [(i + 1, i) for i in range(count - 1)]
    return (
        lax.ppermute(cells[:, -width:], axes, up),
        lax.ppermute(cells[:, :width], axes, down),
    )


def halo_swaps(cells, width):
    axes = ("elem", "sub")
    count = lax.axis_size(axes)
    even = lax.axis_index(axes) % 2 == 0
    tail, head = cells[:, -width:], cells[:, :width]

    def swap(block, first):
        pairs = [(i, i + 1) for i in range(first, count - 1, 2)]
        return lax.ppermute(block, axes, pairs + [(j, i) for i, j in pairs])

    return swap(jnp.where(even, tail, head), 0), swap(jnp.where(even, head, tail), 1)


MEMBER, SLOT, FACE = 1, 2, 3 + FACES


def place_of(z, dest):
    return 3 - (z ^ dest)


def call_plan(count):
    sent = [(p, 0) for p in range(count)]
    kept = [(p, 1) for p in range(count)]
    return [sent[:1], sent[1:] + kept]


def group_lists(elems, count, ints_ref, list_ref, count_ref, call_ref):
    me = lax.axis_index("sub")
    z = lax.axis_index("elem")
    plan = call_plan(count)
    code = {table: (c, t) for c, tables in enumerate(plan) for t, table in enumerate(tables)}
    for d in range(count):
        for x in range(2):
            values = [0, 0]
            for y in range(count):
                for mine in range(2):
                    here = (z == y) & ((me == x) if mine else (me != x))
                    for i in range(2):
                        values[i] = jnp.where(here, code[place_of(y, d), mine][i], values[i])
            call_ref[0, 2 * d + x] = values[0]
            call_ref[1, 2 * d + x] = values[1]
    for call in range(len(plan)):
        count_ref[call] = 0

    def put(e, carry):
        owner = ints_ref[0, e]
        call = call_ref[0, owner]
        at = count_ref[call]
        list_ref[call, at] = 8 * e + call_ref[1, owner]
        count_ref[call] = at + 1
        return carry

    lax.fori_loop(0, elems, put, 0, unroll=4)


def near_kernel(elems, count, ints_ref, cells_ref, other_ref, near_ref, weight_ref, list_ref, count_ref, call_ref):
    group_lists(elems, count, ints_ref, list_ref, count_ref, call_ref)
    near_blocks(near_ref, 0, cells_ref)
    col = lax.axis_index("col")
    own_weights(weight_ref, col, cells_ref)
    own_weights(weight_ref, 1 - col, other_ref)


def rows_kernel(jac_ref, after_ref, rows_ref):
    width = 2048

    def step(i, carry):
        at = pl.ds(pl.multiple_of(i * STEP, STEP), STEP)
        for q in range(jac_ref.shape[1] // width):
            part = jac_ref[at, q * width:(q + 1) * width]
            rows_ref[at, q * 16:(q + 1) * 16] = pltpu.einshape("a(bc)->abc", part, b=16, c=128)
        return carry

    lax.fori_loop(0, jac_ref.shape[0] // STEP, step, 0)


def accumulate(call, trash, rim, ints_ref, list_ref, count_ref, rows_ref, near_ref, weight_ref, total):
    low = lax.broadcasted_iota(jnp.int32, (32, 128), 1) < B
    high = jnp.where(low, 0, 1)
    number = count_ref[call]
    device = lax.axis_index("elem") * lax.axis_size("sub") + lax.axis_index("sub")
    first_row = device * 4 * rim - rim
    absent = near_ref.shape[0] - 1
    total[...] = jnp.zeros_like(total)

    def body(it, carry):
        items = []
        for u in range(UNROLL):
            at = it * UNROLL + u
            valid = at < number
            entry = jnp.where(valid, list_ref[call, at], 0)
            e = entry >> 3
            items.append((valid, e, ints_ref[MEMBER, e] * CS + (entry & (7)) * BLOCKS))
        products = []
        for valid, e, base in items:
            parts = []
            for j in range(FACES + 1):
                if j == 0:
                    cell = e + rim
                else:
                    face = ints_ref[FACE + j - 1, e]
                    cell = jnp.where(face >= 0, face - first_row, absent)
                block = rows_ref[e, j * 32:(j + 1) * 32, :]
                zero = jnp.zeros_like(block)
                weights = jnp.concatenate([jnp.where(low, block, zero), jnp.where(low, zero, block)], axis=0)
                parts.append(lax.dot_general(near_ref[cell], weights, NT, preferred_element_type=jnp.float32))
            products.append(jnp.concatenate(parts, axis=0).astype(jnp.bfloat16))
        results = []
        for (valid, e, base), product in zip(items, products):
            own = weight_ref[e]
            own = jnp.concatenate([own, own], axis=0)
            results.append(lax.dot_general(product, own, NT, preferred_element_type=jnp.float32))
        for (valid, e, base), result in zip(items, results):
            for j in range(FACES + 1):
                target = jnp.where(valid, base + ints_ref[SLOT + j, e], 2 * trash)
                part = result[j * 32:(j + 1) * 32, :]
                total[target >> 1] += jnp.where(high == (target & 1), part, 0.0)
        return carry

    lax.fori_loop(0, (number + UNROLL - 1) // UNROLL, body, 0)


def near_blocks(near_ref, base, cells_ref):
    low = lax.broadcasted_iota(jnp.int32, (32, 128), 1) < B
    for p in range(cells_ref.shape[1] // 128):
        pair = cells_ref[:, p * 128:(p + 1) * 128].astype(jnp.float32)
        turned = pltpu.roll(pair, B, 1)
        near_ref[base + 2 * p] = jnp.where(low, pair, turned).astype(jnp.bfloat16)
        near_ref[base + 2 * p + 1] = jnp.where(low, turned, pair).astype(jnp.bfloat16)


def own_weights(weight_ref, side, cells_ref):
    row = lax.broadcasted_iota(jnp.int32, (128, B), 0)
    col = lax.broadcasted_iota(jnp.int32, (128, B), 1)
    source = 2 * (col % 32) + col // 32
    picks = [jnp.where(row == source + h * B, 1.0, 0.0).astype(jnp.bfloat16) for h in range(2)]
    at = pl.ds(pl.multiple_of(side * 32, 32), 32)
    for p in range(cells_ref.shape[1] // 128):
        pair = cells_ref[:, p * 128:(p + 1) * 128]
        for h in range(2):
            moved = jnp.dot(pair, picks[h], preferred_element_type=jnp.float32)
            weight_ref[2 * p + h, at, :] = moved.astype(jnp.bfloat16)


def first_kernel(elems, ints_ref, list_ref, count_ref, rows_ref, own_ref, weight_ref, one_ref, two_ref,
                 sent_ref, near_ref, total):
    rim = elems // 4
    device = lax.axis_index("elem") * lax.axis_size("sub") + lax.axis_index("sub")
    even = device % 2 == 0
    near_ref[rim:rim + elems] = own_ref[...]
    near_blocks(near_ref, jnp.where(even, rim + elems, 0), one_ref)
    near_blocks(near_ref, jnp.where(even, 0, rim + elems), two_ref)
    near_ref[near_ref.shape[0] - 1] = jnp.zeros((32, 128), jnp.bfloat16)
    accumulate(0, PAIRS, rim, ints_ref, list_ref, count_ref, rows_ref, near_ref, weight_ref, total)
    sent_ref[...] = total[:PAIRS].astype(jnp.bfloat16)


def next_kernel(elems, call, ints_ref, list_ref, count_ref, rows_ref, near_ref, weight_ref, after_ref, *rest):
    outs, total = rest[:-1], rest[-1]
    accumulate(call, len(outs) * PAIRS, elems // 4, ints_ref, list_ref, count_ref, rows_ref, near_ref, weight_ref, total)
    for k, out in enumerate(outs):
        out[...] = total[k * PAIRS:(k + 1) * PAIRS].astype(out.dtype)


def last_kernel(own_ref, across_ref, *rest):
    parts, out_ref, total = rest[:-2], rest[-2], rest[-1]
    total[...] = own_ref[...] + across_ref[...].astype(jnp.float32)
    at = 0
    for part in parts:
        total[at:at + part.shape[0]] += part[...].astype(jnp.float32)
        at = (at + part.shape[0]) % PAIRS
    low = lax.broadcasted_iota(jnp.int32, (32, 128), 1) < B
    for a in range(AGG_DEV):
        first = a * CS // 2
        for q in range(CS // 2):
            if a % 2 == 0:
                out_ref[a, :, q * 128:(q + 1) * 128] = total[first + q]
            else:
                out_ref[a, :, q * 128:(q + 1) * 128] = jnp.where(
                    low, pltpu.roll(total[first + q], B, 1), pltpu.roll(total[first + q + 1], B, 1))
        last = total[first + CS // 2]
        if a % 2 == 1:
            last = pltpu.roll(last, B, 1)
        out_ref[a, :, (CS // 2) * 128:] = last[:, :B]


def dense(jacobian, prolong, face_pattern, owner, member, coarse_slot):
    elems = jacobian.shape[0]
    half = prolong.shape[0]
    count = lax.axis_size("elem")
    rim = elems // 4
    tiles = jacobian.shape[1] // 128
    plan = call_plan(count)
    cost = pl.CostEstimate(flops=1000, bytes_accessed=1000, transcendentals=0)

    other = lax.ppermute(prolong, "col", [(0, 1), (1, 0)])
    one, two = halo_swaps(prolong, rim * B)
    ints = jnp.concatenate([owner.T, member[None], coarse_slot.T, face_pattern.T], axis=0)

    long = pl.CostEstimate(flops=20_000_000_000, bytes_accessed=1000, transcendentals=0)
    own_near, weights, lists, counts = pl.pallas_call(
        functools.partial(near_kernel, elems, count),
        in_specs=[SMEM, VMEM, VMEM],
        out_specs=[VMEM, VMEM, SMEM, SMEM],
        out_shape=[
            jax.ShapeDtypeStruct((elems, half, 2 * B), jnp.bfloat16),
            jax.ShapeDtypeStruct((elems, CB, B), jnp.bfloat16),
            jax.ShapeDtypeStruct((len(plan), elems + UNROLL), jnp.int32),
            jax.ShapeDtypeStruct((len(plan),), jnp.int32),
        ],
        scratch_shapes=[pltpu.SMEM((2, 2 * count), jnp.int32)],
        compiler_params=params(),
        cost_estimate=long,
        name="near",
    )(ints, prolong, other)
    rows = pl.pallas_call(
        rows_kernel,
        in_specs=[VMEM, pl.BlockSpec(memory_space=pl.ANY)],
        out_specs=VMEM,
        out_shape=jax.ShapeDtypeStruct((elems, tiles, 128), jnp.bfloat16),
        compiler_params=params(),
        cost_estimate=cost,
        name="rows",
    )(jacobian, own_near)

    table = (PAIRS, half, 2 * B)
    sent, near = pl.pallas_call(
        functools.partial(first_kernel, elems),
        in_specs=[SMEM] * 3 + [VMEM] * 5,
        out_specs=[VMEM] * 2,
        out_shape=[
            jax.ShapeDtypeStruct(table, jnp.bfloat16),
            jax.ShapeDtypeStruct((elems + 2 * rim + 1, half, 2 * B), jnp.bfloat16),
        ],
        scratch_shapes=[pltpu.VMEM((PAIRS + 1, half, 2 * B), jnp.float32)],
        compiler_params=params(),
        cost_estimate=cost,
        name="first",
    )(ints, lists, counts, rows, own_near, weights, one, two)
    arrived = [lax.ppermute(sent, "sub", [(0, 1), (1, 0)])]

    def summed(p, at, more=None):
        value = kept[p][at] + arrived[p][at].astype(jnp.float32)
        if more is not None:
            value = value + more.astype(jnp.float32)
        return value.astype(jnp.bfloat16)

    def swapped(block, bit):
        return lax.ppermute(block, "elem", [(y, y ^ bit) for y in range(count)])

    halves = [slice(0, PAIRS // 2), slice(PAIRS // 2, PAIRS)]
    kept = {}
    for call in range(1, len(plan)):
        shapes = [jax.ShapeDtypeStruct(table, jnp.float32 if mine else jnp.bfloat16) for p, mine in plan[call]]
        outs = pl.pallas_call(
            functools.partial(next_kernel, elems, call),
            in_specs=[SMEM] * 3 + [VMEM] * 3 + [pl.BlockSpec(memory_space=pl.ANY)],
            out_specs=[VMEM] * len(shapes),
            out_shape=shapes,
            scratch_shapes=[pltpu.VMEM((len(shapes) * PAIRS + 1, half, 2 * B), jnp.float32)],
            compiler_params=params(),
            cost_estimate=long,
            name="next_%d" % call,
        )(ints, lists, counts, rows, near, weights, sent)
        for (p, mine), out in zip(plan[call], outs):
            if mine:
                kept[p] = out
        for (p, mine), out in zip(plan[call], outs):
            if not mine:
                if p > 1:
                    out = lax.optimization_barrier((out, arrived[0]))[0]
                if p > 2:
                    first = [summed(0, at) for at in halves]
                    out = lax.optimization_barrier((out, *first))[0]
                arrived.append(lax.ppermute(out, "sub", [(0, 1), (1, 0)]))

    near_sums = [swapped(block, 1) for block in first]
    second = [summed(1, at, more) for at, more in zip(halves, near_sums)]
    arrived[2] = lax.optimization_barrier((arrived[2], *second))[0]
    far_sums = [swapped(block, 2) for block in second]
    pieces = [slice(i * PAIRS // 3, (i + 1) * PAIRS // 3) for i in range(3)]
    next_sums = [swapped(summed(2, at), 1) for at in pieces]

    coarse = pl.pallas_call(
        last_kernel,
        in_specs=[VMEM] * (4 + len(pieces)),
        out_specs=VMEM,
        out_shape=jax.ShapeDtypeStruct((AGG_DEV, half, CS * CB), jnp.float32),
        scratch_shapes=[pltpu.VMEM(table, jnp.float32)],
        compiler_params=params(),
        cost_estimate=cost,
        name="last",
    )(kept[count - 1], arrived[count - 1], *next_sums, *far_sums)
    return coarse.transpose(1, 0, 2)


def direct(jacobian, prolong, face_pattern, owner, member, coarse_slot):
    elems = jacobian.shape[0]
    owners = lax.axis_size(("elem", "sub"))
    capacity = max(2, 2 * elems // owners)
    device = lax.axis_index(("elem", "sub"))
    half = prolong.shape[0]
    rim = elems // 4
    before, after = halo(prolong, rim * B)
    ghosts = jnp.concatenate([before, prolong, after], axis=1).reshape(half, elems + 2 * rim, B)
    whole = lax.all_gather(prolong, "col", axis=0, tiled=True).reshape(CB, elems, B)
    first_row = device * elems - rim
    selfcol = jnp.arange(elems, dtype=jnp.int32)[:, None] + rim
    remote = jnp.where(face_pattern >= 0, face_pattern - first_row, 0)
    columns = jnp.concatenate([selfcol, remote], axis=1)
    present = jnp.concatenate([jnp.ones((elems, 1), jnp.bool_), face_pattern >= 0], axis=1)
    neighbour_rows = ghosts[:, columns, :] * present[None, :, :, None].astype(jnp.bfloat16)
    blocks = jacobian.reshape(elems, FACES + 1, B, B)
    product = jnp.einsum(
        "ejik,cejk->ejic", blocks, neighbour_rows, preferred_element_type=jnp.float32
    ).astype(jnp.bfloat16)
    owner_flat = owner[:, 0]
    marks = (owner_flat[:, None] == jnp.arange(owners, dtype=jnp.int32)[None, :]).astype(jnp.int32)
    ranking = jnp.sum(jnp.cumsum(marks, axis=0) * marks, axis=1) - 1
    place = owner_flat * capacity + ranking
    target = member[:, None] * CS + coarse_slot
    slots = owners * capacity
    labels = jnp.full((slots, FACES + 1), -1, jnp.int32).at[place].set(target)
    contribution = jnp.einsum("rei,ejic->ejcr", whole, product, preferred_element_type=jnp.float32)
    payload = jnp.zeros((slots, FACES + 1, half, CB), jnp.float32).at[place].set(contribution)
    axes = ("elem", "sub")
    arrived = lax.all_to_all(payload, axes, split_axis=0, concat_axis=0, tiled=True)
    arrived_labels = lax.all_to_all(labels, axes, split_axis=0, concat_axis=0, tiled=True)
    items = slots * (FACES + 1)
    values = arrived.reshape(items, half * CB)
    flat_labels = arrived_labels.reshape(items)
    destination = jnp.where(flat_labels >= 0, flat_labels, BLOCKS).astype(jnp.int32)
    summed = jnp.zeros((BLOCKS, half * CB), jnp.float32).at[destination].add(values, mode="drop")
    summed = summed.reshape(AGG_DEV, CS, half, CB).transpose(2, 0, 1, 3)
    return summed.reshape(half, AGG_DEV, CS * CB)


def shards(jacobian, *rest):
    elems = jacobian.shape[0]
    owners = lax.axis_size(("elem", "sub"))
    capacity = max(2, 2 * elems // owners)
    if lax.axis_size("sub") == 2 and lax.axis_size("elem") == 4 and BLOCKS <= capacity * (FACES + 1):
        return dense(jacobian, *rest)
    return direct(jacobian, *rest)


def solution(mesh):
    in_specs = (
        P(("groups", "elem", "sub"), None),
        P("col", ("groups", "elem", "sub")),
        P(("groups", "elem", "sub"), None),
        P(("groups", "elem", "sub"), None),
        P(("groups", "elem", "sub")),
        P(("groups", "elem", "sub"), None),
    )
    out_specs = P("col", ("groups", "elem", "sub"), None)
    return jax.shard_map(shards, mesh=mesh, in_specs=in_specs, out_specs=out_specs, check_vma=False)
```

```python
import functools

import jax
import jax.numpy as jnp
from jax import lax
from jax.experimental import pallas as pl
from jax.experimental.pallas import tpu as pltpu
from jax.sharding import PartitionSpec as P

B = 64
CB = 64
FACES = 4
CS = 9
AGG_DEV = 12
BLOCKS = AGG_DEV * CS
PAIRS = BLOCKS // 2
STEP = 16
UNROLL = 8
VMEM = pl.BlockSpec(memory_space=pltpu.VMEM)
SMEM = pl.BlockSpec(memory_space=pltpu.SMEM)
NT = (((1,), (1,)), ((), ()))


def params(mib=16):
    return pltpu.CompilerParams(vmem_limit_bytes=mib * 1024 * 1024)


def halo(cells, width):
    axes = ("elem", "sub")
    count = lax.axis_size(axes)
    up = [(i, i + 1) for i in range(count - 1)]
    down = [(i + 1, i) for i in range(count - 1)]
    return (
        lax.ppermute(cells[:, -width:], axes, up),
        lax.ppermute(cells[:, :width], axes, down),
    )


def halo_swaps(cells, width):
    axes = ("elem", "sub")
    count = lax.axis_size(axes)
    even = lax.axis_index(axes) % 2 == 0
    tail, head = cells[:, -width:], cells[:, :width]

    def swap(block, first):
        pairs = [(i, i + 1) for i in range(first, count - 1, 2)]
        return lax.ppermute(block, axes, pairs + [(j, i) for i, j in pairs])

    return swap(jnp.where(even, tail, head), 0), swap(jnp.where(even, head, tail), 1)


MEMBER, SLOT, FACE = 1, 2, 3 + FACES
CELL, TARGET = 0, FACES
LANES = 128


ROUNDS = ([(0, 2), (1, 0), (2, 3), (3, 1)], [(0, 1), (1, 3), (2, 0), (3, 2)])


def place_of(z, dest):
    if dest in (z, z ^ 3):
        return 3 if dest == z else 0
    return 1 if (z, dest) in ROUNDS[0] else 2


def call_plan(count):
    sent = [(p, 0) for p in range(count)]
    kept = [(p, 1) for p in range(count)]
    return [sent[:2], sent[2:] + kept]


def group_lists(elems, count, ints_ref, list_ref, count_ref, call_ref):
    me = lax.axis_index("sub")
    z = lax.axis_index("elem")
    plan = call_plan(count)
    code = {table: (c, 2 + t * BLOCKS) for c, tables in enumerate(plan) for t, table in enumerate(tables)}
    for d in range(count):
        for x in range(2):
            values = [0, 0]
            for y in range(count):
                for mine in range(2):
                    here = (z == y) & ((me == x) if mine else (me != x))
                    for i in range(2):
                        values[i] = jnp.where(here, code[place_of(y, d), mine][i], values[i])
            call_ref[0, 2 * d + x] = values[0]
            call_ref[1, 2 * d + x] = LANES * values[1]
    for call in range(len(plan)):
        count_ref[call] = 0

    def put(e, carry):
        owner = ints_ref[0, e]
        call = call_ref[0, owner]
        at = count_ref[call]
        list_ref[call, at] = e + call_ref[1, owner]
        count_ref[call] = at + 1
        return carry

    lax.fori_loop(0, elems, put, 0, unroll=8)
    for call in range(len(plan)):
        for u in range(UNROLL):
            list_ref[call, count_ref[call] + u] = elems


def near_kernel(elems, count, ints_ref, again_ref, cells_ref, other_ref,
                near_ref, weight_ref, code_ref, list_ref, count_ref, call_ref):
    device = lax.axis_index("elem") * lax.axis_size("sub") + lax.axis_index("sub")
    rim = elems // 4
    faces = again_ref[FACE:FACE + FACES, :]
    code_ref[...] = jnp.zeros_like(code_ref)
    code_ref[CELL:CELL + FACES, :elems] = jnp.where(faces >= 0, faces - (device * elems - rim), elems + 2 * rim)
    code_ref[TARGET:TARGET + FACES + 1, :elems] = (
        again_ref[MEMBER:MEMBER + 1, :] * CS + again_ref[SLOT:SLOT + FACES + 1, :])
    group_lists(elems, count, ints_ref, list_ref, count_ref, call_ref)
    near_blocks(near_ref, 0, cells_ref)
    col = lax.axis_index("col")
    own_weights(weight_ref, col, cells_ref)
    own_weights(weight_ref, 1 - col, other_ref)


def rows_kernel(jac_ref, after_ref, rows_ref):
    width = 2048

    def step(i, carry):
        at = pl.ds(pl.multiple_of(i * STEP, STEP), STEP)
        for q in range(jac_ref.shape[1] // width):
            part = jac_ref[at, q * width:(q + 1) * width]
            rows_ref[at, q * 16:(q + 1) * 16] = pltpu.einshape("a(bc)->abc", part, b=16, c=128)
        return carry

    lax.fori_loop(0, jac_ref.shape[0] // STEP, step, 0)


def accumulate(call, elems, code_ref, list_ref, count_ref, rows_ref, near_ref, weight_ref, total):
    low = lax.broadcasted_iota(jnp.int32, (32, 128), 1) < B
    high = jnp.where(low, 0, 1)
    total[...] = jnp.zeros_like(total)

    def body(it, carry):
        items = []
        for u in range(UNROLL):
            entry = list_ref[call, it * UNROLL + u]
            at = entry & (LANES - 1)
            items.append((at, jnp.minimum(at, elems - 1), entry >> 7))
        products = []
        for at, e, base in items:
            parts = []
            for j in range(FACES + 1):
                cell = near_ref[e + elems // 4 if j == 0 else code_ref[CELL + j - 1, at]]
                zero = jnp.zeros_like(cell)
                both = jnp.concatenate([jnp.where(low, cell, zero), jnp.where(low, zero, cell)], axis=0)
                block = rows_ref[e, j * 32:(j + 1) * 32, :]
                part = lax.dot_general(both, block, NT, preferred_element_type=jnp.float32)
                parts.append(jnp.concatenate([part[:32], part[32:]], axis=1))
            products.append(jnp.concatenate(parts, axis=0).astype(jnp.bfloat16))
        results = []
        for (at, e, base), product in zip(items, products):
            own = weight_ref[e]
            own = jnp.concatenate([own, own], axis=0)
            results.append(lax.dot_general(product, own, NT, preferred_element_type=jnp.float32))
        for (at, e, base), result in zip(items, results):
            for j in range(FACES + 1):
                target = base + code_ref[TARGET + j, at]
                part = result[j * 32:(j + 1) * 32, :]
                total[target >> 1] += jnp.where(high == (target & 1), part, 0.0)
        return carry

    lax.fori_loop(0, (count_ref[call] + UNROLL - 1) // UNROLL, body, 0)


def near_blocks(near_ref, base, cells_ref):
    low = lax.broadcasted_iota(jnp.int32, (32, 128), 1) < B
    for p in range(cells_ref.shape[1] // 128):
        pair = cells_ref[:, p * 128:(p + 1) * 128].astype(jnp.float32)
        turned = pltpu.roll(pair, B, 1)
        near_ref[base + 2 * p] = jnp.where(low, pair, turned).astype(jnp.bfloat16)
        near_ref[base + 2 * p + 1] = jnp.where(low, turned, pair).astype(jnp.bfloat16)


def own_weights(weight_ref, side, cells_ref):
    row = lax.broadcasted_iota(jnp.int32, (128, B), 0)
    col = lax.broadcasted_iota(jnp.int32, (128, B), 1)
    source = 2 * (col % 32) + col // 32
    picks = [jnp.where(row == source + h * B, 1.0, 0.0).astype(jnp.bfloat16) for h in range(2)]
    at = pl.ds(pl.multiple_of(side * 32, 32), 32)
    for p in range(cells_ref.shape[1] // 128):
        pair = cells_ref[:, p * 128:(p + 1) * 128]
        for h in range(2):
            moved = jnp.dot(pair, picks[h], preferred_element_type=jnp.float32)
            weight_ref[2 * p + h, at, :] = moved.astype(jnp.bfloat16)


def first_kernel(elems, code_ref, list_ref, count_ref, rows_ref, own_ref, weight_ref, one_ref, two_ref, *rest):
    outs, near_ref, total = rest[:-2], rest[-2], rest[-1]
    rim = elems // 4
    device = lax.axis_index("elem") * lax.axis_size("sub") + lax.axis_index("sub")
    even = device % 2 == 0
    near_ref[rim:rim + elems] = own_ref[...]
    near_blocks(near_ref, jnp.where(even, rim + elems, 0), one_ref)
    near_blocks(near_ref, jnp.where(even, 0, rim + elems), two_ref)
    near_ref[near_ref.shape[0] - 1] = jnp.zeros((32, 128), jnp.bfloat16)
    accumulate(0, elems, code_ref, list_ref, count_ref, rows_ref, near_ref, weight_ref, total)
    for k, out in enumerate(outs):
        out[...] = total[1 + k * PAIRS:1 + (k + 1) * PAIRS].astype(out.dtype)


def next_kernel(elems, call, code_ref, list_ref, count_ref, rows_ref, near_ref, weight_ref, *rest):
    outs, total = rest[:-1], rest[-1]
    accumulate(call, elems, code_ref, list_ref, count_ref, rows_ref, near_ref, weight_ref, total)
    for k, out in enumerate(outs):
        out[...] = total[1 + k * PAIRS:1 + (k + 1) * PAIRS].astype(out.dtype)


def last_kernel(own_ref, across_ref, *rest):
    parts, out_ref, total = rest[:-2], rest[-2], rest[-1]
    total[...] = own_ref[...] + across_ref[...].astype(jnp.float32)
    at = 0
    for part in parts:
        total[at:at + part.shape[0]] += part[...].astype(jnp.float32)
        at = (at + part.shape[0]) % PAIRS
    low = lax.broadcasted_iota(jnp.int32, (32, 128), 1) < B
    for a in range(AGG_DEV):
        first = a * CS // 2
        for q in range(CS // 2):
            if a % 2 == 0:
                out_ref[a, :, q * 128:(q + 1) * 128] = total[first + q]
            else:
                out_ref[a, :, q * 128:(q + 1) * 128] = jnp.where(
                    low, pltpu.roll(total[first + q], B, 1), pltpu.roll(total[first + q + 1], B, 1))
        last = total[first + CS // 2]
        if a % 2 == 1:
            last = pltpu.roll(last, B, 1)
        out_ref[a, :, (CS // 2) * 128:] = last[:, :B]


def dense(jacobian, prolong, face_pattern, owner, member, coarse_slot):
    elems = jacobian.shape[0]
    half = prolong.shape[0]
    count = lax.axis_size("elem")
    rim = elems // 4
    tiles = jacobian.shape[1] // 128
    plan = call_plan(count)
    cost = pl.CostEstimate(flops=1000, bytes_accessed=1000, transcendentals=0)

    other = lax.ppermute(prolong, "col", [(0, 1), (1, 0)])
    one, two = halo_swaps(prolong, rim * B)
    ints = jnp.concatenate([owner.T, member[None], coarse_slot.T, face_pattern.T], axis=0)

    long = pl.CostEstimate(flops=20_000_000_000, bytes_accessed=1000, transcendentals=0)
    own_near, weights, codes, lists, counts = pl.pallas_call(
        functools.partial(near_kernel, elems, count),
        in_specs=[SMEM, VMEM, VMEM, VMEM],
        out_specs=[VMEM, VMEM, VMEM, SMEM, SMEM],
        out_shape=[
            jax.ShapeDtypeStruct((elems, half, 2 * B), jnp.bfloat16),
            jax.ShapeDtypeStruct((elems, CB, B), jnp.bfloat16),
            jax.ShapeDtypeStruct((16, LANES), jnp.int32),
            jax.ShapeDtypeStruct((len(plan), elems + UNROLL), jnp.int32),
            jax.ShapeDtypeStruct((len(plan),), jnp.int32),
        ],
        scratch_shapes=[pltpu.SMEM((2, 2 * count), jnp.int32)],
        compiler_params=params(),
        cost_estimate=long,
        name="near",
    )(ints, ints, prolong, other)
    rows = pl.pallas_call(
        rows_kernel,
        in_specs=[VMEM, pl.BlockSpec(memory_space=pl.ANY)],
        out_specs=VMEM,
        out_shape=jax.ShapeDtypeStruct((elems, tiles, 128), jnp.bfloat16),
        compiler_params=params(),
        cost_estimate=cost,
        name="rows",
    )(jacobian, own_near)

    table = (PAIRS, half, 2 * B)
    *sent, near = pl.pallas_call(
        functools.partial(first_kernel, elems),
        in_specs=[SMEM] * 3 + [VMEM] * 5,
        out_specs=[VMEM] * 3,
        out_shape=[jax.ShapeDtypeStruct(table, jnp.bfloat16)] * 2 + [
            jax.ShapeDtypeStruct((elems + 2 * rim + 1, half, 2 * B), jnp.bfloat16),
        ],
        scratch_shapes=[pltpu.VMEM((1 + 2 * PAIRS, half, 2 * B), jnp.float32)],
        compiler_params=params(),
        cost_estimate=cost,
        name="first",
    )(codes, lists, counts, rows, own_near, weights, one, two)
    arrived = [lax.ppermute(block, "sub", [(0, 1), (1, 0)]) for block in sent]

    outer = (lax.axis_index("elem") + 1) % 4 < 2

    def summed(p, at, more=None, adds=None):
        value = kept[p][at] + arrived[p][at].astype(jnp.float32)
        if more is not None:
            value = value + jnp.where(adds, more.astype(jnp.float32), 0.0)
        return value.astype(jnp.bfloat16)

    def sent_to(block, pairs):
        return lax.ppermute(block, "elem", pairs)

    halves = [slice(0, PAIRS // 2), slice(PAIRS // 2, PAIRS)]
    shapes = [jax.ShapeDtypeStruct(table, jnp.float32 if mine else jnp.bfloat16) for p, mine in plan[1]]
    outs = pl.pallas_call(
        functools.partial(next_kernel, elems, 1),
        in_specs=[SMEM] * 3 + [VMEM] * 3,
        out_specs=[VMEM] * len(shapes),
        out_shape=shapes,
        scratch_shapes=[pltpu.VMEM((1 + len(shapes) * PAIRS, half, 2 * B), jnp.float32)],
        compiler_params=params(),
        cost_estimate=long,
        name="next",
    )(codes, lists, counts, rows, near, weights)
    sent, kept = outs[:count - 2], outs[count - 2:]
    first = [summed(0, at) for at in halves]
    for block in sent:
        block = lax.optimization_barrier((block, *first))[0]
        arrived.append(lax.ppermute(block, "sub", [(0, 1), (1, 0)]))

    near_sums = [sent_to(block, [(y, y ^ 1) for y in range(count)]) for block in first]
    near_sums = jnp.concatenate(near_sums, axis=0)
    second = summed(1, slice(None), near_sums, outer)
    arrived[2] = lax.optimization_barrier((arrived[2], second))[0]
    parts = [sent_to(second, ROUNDS[0])]
    parts += [sent_to(summed(2, at, near_sums[at], ~outer), ROUNDS[1]) for at in halves]

    coarse = pl.pallas_call(
        last_kernel,
        in_specs=[VMEM] * 5,
        out_specs=VMEM,
        out_shape=jax.ShapeDtypeStruct((AGG_DEV, half, CS * CB), jnp.float32),
        scratch_shapes=[pltpu.VMEM(table, jnp.float32)],
        compiler_params=params(),
        cost_estimate=cost,
        name="last",
    )(kept[count - 1], arrived[count - 1], *parts)
    return coarse.transpose(1, 0, 2)


def direct(jacobian, prolong, face_pattern, owner, member, coarse_slot):
    elems = jacobian.shape[0]
    owners = lax.axis_size(("elem", "sub"))
    capacity = max(2, 2 * elems // owners)
    device = lax.axis_index(("elem", "sub"))
    half = prolong.shape[0]
    rim = elems // 4
    before, after = halo(prolong, rim * B)
    ghosts = jnp.concatenate([before, prolong, after], axis=1).reshape(half, elems + 2 * rim, B)
    whole = lax.all_gather(prolong, "col", axis=0, tiled=True).reshape(CB, elems, B)
    first_row = device * elems - rim
    selfcol = jnp.arange(elems, dtype=jnp.int32)[:, None] + rim
    remote = jnp.where(face_pattern >= 0, face_pattern - first_row, 0)
    columns = jnp.concatenate([selfcol, remote], axis=1)
    present = jnp.concatenate([jnp.ones((elems, 1), jnp.bool_), face_pattern >= 0], axis=1)
    neighbour_rows = ghosts[:, columns, :] * present[None, :, :, None].astype(jnp.bfloat16)
    blocks = jacobian.reshape(elems, FACES + 1, B, B)
    product = jnp.einsum(
        "ejik,cejk->ejic", blocks, neighbour_rows, preferred_element_type=jnp.float32
    ).astype(jnp.bfloat16)
    owner_flat = owner[:, 0]
    marks = (owner_flat[:, None] == jnp.arange(owners, dtype=jnp.int32)[None, :]).astype(jnp.int32)
    ranking = jnp.sum(jnp.cumsum(marks, axis=0) * marks, axis=1) - 1
    place = owner_flat * capacity + ranking
    target = member[:, None] * CS + coarse_slot
    slots = owners * capacity
    labels = jnp.full((slots, FACES + 1), -1, jnp.int32).at[place].set(target)
    contribution = jnp.einsum("rei,ejic->ejcr", whole, product, preferred_element_type=jnp.float32)
    payload = jnp.zeros((slots, FACES + 1, half, CB), jnp.float32).at[place].set(contribution)
    axes = ("elem", "sub")
    arrived = lax.all_to_all(payload, axes, split_axis=0, concat_axis=0, tiled=True)
    arrived_labels = lax.all_to_all(labels, axes, split_axis=0, concat_axis=0, tiled=True)
    items = slots * (FACES + 1)
    values = arrived.reshape(items, half * CB)
    flat_labels = arrived_labels.reshape(items)
    destination = jnp.where(flat_labels >= 0, flat_labels, BLOCKS).astype(jnp.int32)
    summed = jnp.zeros((BLOCKS, half * CB), jnp.float32).at[destination].add(values, mode="drop")
    summed = summed.reshape(AGG_DEV, CS, half, CB).transpose(2, 0, 1, 3)
    return summed.reshape(half, AGG_DEV, CS * CB)


def shards(jacobian, *rest):
    elems = jacobian.shape[0]
    owners = lax.axis_size(("elem", "sub"))
    capacity = max(2, 2 * elems // owners)
    if lax.axis_size("sub") == 2 and lax.axis_size("elem") == 4 and BLOCKS <= capacity * (FACES + 1):
        return dense(jacobian, *rest)
    return direct(jacobian, *rest)


def solution(mesh):
    in_specs = (
        P(("groups", "elem", "sub"), None),
        P("col", ("groups", "elem", "sub")),
        P(("groups", "elem", "sub"), None),
        P(("groups", "elem", "sub"), None),
        P(("groups", "elem", "sub")),
        P(("groups", "elem", "sub"), None),
    )
    out_specs = P("col", ("groups", "elem", "sub"), None)
    return jax.shard_map(shards, mesh=mesh, in_specs=in_specs, out_specs=out_specs, check_vma=False)
```

```python
import functools

import jax
import jax.numpy as jnp
from jax import lax
from jax.experimental import pallas as pl
from jax.experimental.pallas import tpu as pltpu
from jax.sharding import PartitionSpec as P

B = 64
CB = 64
FACES = 4
CS = 9
AGG_DEV = 12
BLOCKS = AGG_DEV * CS
PAIRS = BLOCKS // 2
STEP = 16
UNROLL = 8
VMEM = pl.BlockSpec(memory_space=pltpu.VMEM)
SMEM = pl.BlockSpec(memory_space=pltpu.SMEM)
NT = (((1,), (1,)), ((), ()))


def params(mib=16):
    return pltpu.CompilerParams(vmem_limit_bytes=mib * 1024 * 1024)


def halo(cells, width):
    axes = ("elem", "sub")
    count = lax.axis_size(axes)
    up = [(i, i + 1) for i in range(count - 1)]
    down = [(i + 1, i) for i in range(count - 1)]
    return (
        lax.ppermute(cells[:, -width:], axes, up),
        lax.ppermute(cells[:, :width], axes, down),
    )


def halo_swaps(cells, width):
    axes = ("elem", "sub")
    count = lax.axis_size(axes)
    even = lax.axis_index(axes) % 2 == 0
    tail, head = cells[:, -width:], cells[:, :width]

    def swap(block, first):
        pairs = [(i, i + 1) for i in range(first, count - 1, 2)]
        return lax.ppermute(block, axes, pairs + [(j, i) for i, j in pairs])

    return swap(jnp.where(even, tail, head), 0), swap(jnp.where(even, head, tail), 1)


MEMBER, SLOT, FACE = 1, 2, 3 + FACES
CELL, TARGET = 0, FACES
LANES = 128


ROUNDS = ([(0, 2), (1, 0), (2, 3), (3, 1)], [(0, 1), (1, 3), (2, 0), (3, 2)])


def place_of(z, dest):
    if dest in (z, z ^ 3):
        return 3 if dest == z else 0
    return 1 if (z, dest) in ROUNDS[0] else 2


def call_plan(count):
    sent = [(p, 0) for p in range(count)]
    kept = [(p, 1) for p in range(count)]
    return [sent[:1], sent[1:] + kept]


def lists_kernel(elems, count, ints_ref, again_ref, code_ref, list_ref, count_ref):
    me = lax.axis_index("sub")
    z = lax.axis_index("elem")
    plan = call_plan(count)
    code = {table: (c, t) for c, tables in enumerate(plan) for t, table in enumerate(tables)}
    numbers, calls = 0, 0
    for d in range(count):
        for x in range(2):
            values = [0, 0]
            for y in range(count):
                for mine in range(2):
                    here = (z == y) & ((me == x) if mine else (me != x))
                    for i in range(2):
                        values[i] = jnp.where(here, code[place_of(y, d), mine][i], values[i])
            calls += values[0] << (2 * d + x)
            numbers += values[1] << (3 * (2 * d + x))

    device = z * lax.axis_size("sub") + me
    rim = elems // 4
    faces = again_ref[FACE:FACE + FACES, :]
    code_ref[...] = jnp.zeros_like(code_ref)
    code_ref[CELL:CELL + FACES, :elems] = jnp.where(faces >= 0, faces - (device * elems - rim), elems + 2 * rim)
    code_ref[TARGET:TARGET + FACES + 1, :elems] = (
        again_ref[MEMBER:MEMBER + 1, :] * CS + again_ref[SLOT:SLOT + FACES + 1, :])

    zero, one = 0, 0
    for start in range(0, elems, STEP):
        owners = [ints_ref[0, e] for e in range(start, start + STEP)]
        for e, owner in zip(range(start, start + STEP), owners):
            call = (calls >> owner) & 1
            number = (numbers >> (3 * owner)) & 7
            list_ref[call, jnp.where(call == 0, zero, one)] = LANES * BLOCKS * number + (2 * LANES + e)
            zero, one = zero + 1 - call, one + call
    for call, number in enumerate((zero, one)):
        count_ref[call] = number
        for u in range(UNROLL):
            list_ref[call, number + u] = elems


def near_kernel(cells_ref, other_ref, after_ref, near_ref, weight_ref):
    near_blocks(near_ref, 0, cells_ref)
    own_weights(weight_ref, cells_ref, other_ref)


def rows_kernel(jac_ref, after_ref, rows_ref):
    width = 2048

    def step(i, carry):
        at = pl.ds(pl.multiple_of(i * STEP, STEP), STEP)
        for q in range(jac_ref.shape[1] // width):
            part = jac_ref[at, q * width:(q + 1) * width]
            rows_ref[at, q * 16:(q + 1) * 16] = pltpu.einshape("a(bc)->abc", part, b=16, c=128)
        return carry

    lax.fori_loop(0, jac_ref.shape[0] // STEP, step, 0)


def accumulate(call, elems, code_ref, list_ref, count_ref, rows_ref, near_ref, weight_ref, total):
    low = lax.broadcasted_iota(jnp.int32, (32, 128), 1) < B
    high = jnp.where(low, 0, 1)
    total[...] = jnp.zeros_like(total)

    def body(it, carry):
        items = []
        for u in range(UNROLL):
            entry = list_ref[call, it * UNROLL + u]
            at = entry & (LANES - 1)
            items.append((at, jnp.minimum(at, elems - 1), entry >> 7))
        products = []
        for at, e, base in items:
            parts = []
            for j in range(FACES + 1):
                cell = near_ref[e + elems // 4 if j == 0 else code_ref[CELL + j - 1, at]]
                zero = jnp.zeros_like(cell)
                both = jnp.concatenate([jnp.where(low, cell, zero), jnp.where(low, zero, cell)], axis=0)
                block = rows_ref[e, j * 32:(j + 1) * 32, :]
                part = lax.dot_general(both, block, NT, preferred_element_type=jnp.float32)
                parts.append(jnp.concatenate([part[:32], part[32:]], axis=1))
            products.append(jnp.concatenate(parts, axis=0).astype(jnp.bfloat16))
        results = []
        for (at, e, base), product in zip(items, products):
            own = weight_ref[e]
            own = jnp.concatenate([own, own], axis=0)
            results.append(lax.dot_general(product, own, NT, preferred_element_type=jnp.float32))
        for (at, e, base), result in zip(items, results):
            for j in range(FACES + 1):
                target = base + code_ref[TARGET + j, at]
                part = result[j * 32:(j + 1) * 32, :]
                total[target >> 1] += jnp.where(high == (target & 1), part, 0.0)
        return carry

    lax.fori_loop(0, (count_ref[call] + UNROLL - 1) // UNROLL, body, 0)


def near_blocks(near_ref, base, cells_ref):
    low = lax.broadcasted_iota(jnp.int32, (32, 128), 1) < B
    for p in range(cells_ref.shape[1] // 128):
        pair = cells_ref[:, p * 128:(p + 1) * 128].astype(jnp.float32)
        turned = pltpu.roll(pair, B, 1)
        near_ref[base + 2 * p] = jnp.where(low, pair, turned).astype(jnp.bfloat16)
        near_ref[base + 2 * p + 1] = jnp.where(low, turned, pair).astype(jnp.bfloat16)


def own_weights(weight_ref, cells_ref, other_ref):
    row = lax.broadcasted_iota(jnp.int32, (128, 128), 0)
    col = lax.broadcasted_iota(jnp.int32, (128, 128), 1)
    source = (col // B) * B + 2 * (col % 32) + (col % B) // 32
    pick = jnp.where(row == source, 1.0, 0.0).astype(jnp.bfloat16)
    low_first = lax.axis_index("col") == 0
    step = 8
    for p in range(0, cells_ref.shape[1] // 128, step):
        stacked = []
        for q in range(p, p + step):
            own, other = cells_ref[:, q * 128:(q + 1) * 128], other_ref[:, q * 128:(q + 1) * 128]
            stacked += [jnp.where(low_first, own, other), jnp.where(low_first, other, own)]
        moved = jnp.dot(jnp.concatenate(stacked, axis=0), pick, preferred_element_type=jnp.float32)
        for q in range(step):
            pair = moved[q * CB:(q + 1) * CB]
            for h in range(2):
                weight_ref[2 * (p + q) + h] = pair[:, h * B:(h + 1) * B].astype(jnp.bfloat16)


def first_kernel(elems, code_ref, list_ref, count_ref, rows_ref, own_ref, weight_ref, one_ref, two_ref, *rest):
    outs, near_ref, total = rest[:-2], rest[-2], rest[-1]
    rim = elems // 4
    device = lax.axis_index("elem") * lax.axis_size("sub") + lax.axis_index("sub")
    even = device % 2 == 0
    near_ref[rim:rim + elems] = own_ref[...]
    near_blocks(near_ref, jnp.where(even, rim + elems, 0), one_ref)
    near_blocks(near_ref, jnp.where(even, 0, rim + elems), two_ref)
    near_ref[near_ref.shape[0] - 1] = jnp.zeros((32, 128), jnp.bfloat16)
    accumulate(0, elems, code_ref, list_ref, count_ref, rows_ref, near_ref, weight_ref, total)
    for k, out in enumerate(outs):
        out[...] = total[1 + k * PAIRS:1 + (k + 1) * PAIRS].astype(out.dtype)


def next_kernel(elems, call, cuts, code_ref, list_ref, count_ref, rows_ref, near_ref, weight_ref, *rest):
    outs, total = rest[:-1], rest[-1]
    accumulate(call, elems, code_ref, list_ref, count_ref, rows_ref, near_ref, weight_ref, total)
    for (t, at), out in zip(cuts, outs):
        start = 1 + t * PAIRS
        out[...] = total[start + at.start:start + at.stop].astype(out.dtype)


def add_kernel(start, kept_ref, came_ref, *rest):
    out_ref = rest[-1]
    at = slice(start, start + out_ref.shape[0])
    value = kept_ref[at] + came_ref[...].astype(jnp.float32)
    for more_ref in rest[:-1]:
        value = value + more_ref[at].astype(jnp.float32)
    out_ref[...] = value.astype(out_ref.dtype)


def gather_kernel(own_ref, *rest):
    parts, total = rest[:-1], rest[-1]
    total[...] = own_ref[...]
    at = 0
    for part in parts:
        total[at:at + part.shape[0]] += part[...].astype(jnp.float32)
        at = (at + part.shape[0]) % PAIRS


def last_kernel(*rest):
    out_ref, total = rest[-2], rest[-1]
    gather_kernel(*rest[:-2], total)
    low = lax.broadcasted_iota(jnp.int32, (32, 128), 1) < B
    for a in range(AGG_DEV):
        first = a * CS // 2
        for q in range(CS // 2):
            if a % 2 == 0:
                out_ref[a, :, q * 128:(q + 1) * 128] = total[first + q]
            else:
                out_ref[a, :, q * 128:(q + 1) * 128] = jnp.where(
                    low, pltpu.roll(total[first + q], B, 1), pltpu.roll(total[first + q + 1], B, 1))
        last = total[first + CS // 2]
        if a % 2 == 1:
            last = pltpu.roll(last, B, 1)
        out_ref[a, :, (CS // 2) * 128:] = last[:, :B]


def dense(jacobian, prolong, face_pattern, owner, member, coarse_slot):
    elems = jacobian.shape[0]
    half = prolong.shape[0]
    count = lax.axis_size("elem")
    rim = elems // 4
    tiles = jacobian.shape[1] // 128
    plan = call_plan(count)
    cost = pl.CostEstimate(flops=1000, bytes_accessed=1000, transcendentals=0)

    other = lax.ppermute(prolong, "col", [(0, 1), (1, 0)])
    one, two = halo_swaps(prolong, rim * B)
    ints = jnp.concatenate([owner.T, member[None], coarse_slot.T, face_pattern.T], axis=0)

    long = pl.CostEstimate(flops=20_000_000_000, bytes_accessed=1000, transcendentals=0)
    codes, lists, counts = pl.pallas_call(
        functools.partial(lists_kernel, elems, count),
        in_specs=[SMEM, VMEM],
        out_specs=[VMEM, SMEM, SMEM],
        out_shape=[
            jax.ShapeDtypeStruct((16, LANES), jnp.int32),
            jax.ShapeDtypeStruct((len(plan), elems + UNROLL), jnp.int32),
            jax.ShapeDtypeStruct((len(plan),), jnp.int32),
        ],
        compiler_params=params(),
        cost_estimate=long,
        name="lists",
    )(ints, ints)
    own_near, weights = pl.pallas_call(
        near_kernel,
        in_specs=[VMEM, VMEM, pl.BlockSpec(memory_space=pl.ANY)],
        out_specs=[VMEM, VMEM],
        out_shape=[
            jax.ShapeDtypeStruct((elems, half, 2 * B), jnp.bfloat16),
            jax.ShapeDtypeStruct((elems, CB, B), jnp.bfloat16),
        ],
        compiler_params=params(),
        cost_estimate=cost,
        name="near",
    )(prolong, other, codes)
    rows = pl.pallas_call(
        rows_kernel,
        in_specs=[VMEM, pl.BlockSpec(memory_space=pl.ANY)],
        out_specs=VMEM,
        out_shape=jax.ShapeDtypeStruct((elems, tiles, 128), jnp.bfloat16),
        compiler_params=params(),
        cost_estimate=cost,
        name="rows",
    )(jacobian, own_near)

    table = (PAIRS, half, 2 * B)
    sent, near = pl.pallas_call(
        functools.partial(first_kernel, elems),
        in_specs=[SMEM] * 3 + [VMEM] * 5,
        out_specs=[VMEM] * 2,
        out_shape=[
            jax.ShapeDtypeStruct(table, jnp.bfloat16),
            jax.ShapeDtypeStruct((elems + 2 * rim + 1, half, 2 * B), jnp.bfloat16),
        ],
        scratch_shapes=[pltpu.VMEM((1 + PAIRS, half, 2 * B), jnp.float32)],
        compiler_params=params(),
        cost_estimate=cost,
        name="first",
    )(codes, lists, counts, rows, own_near, weights, one, two)

    def across(block):
        return lax.ppermute(block, "sub", [(0, 1), (1, 0)])

    def along(block, pairs):
        return lax.ppermute(block, "elem", pairs)

    def behind(block, *others):
        return lax.optimization_barrier((block, *others))[0]

    def summed(p, at, block, *more):
        return pl.pallas_call(
            functools.partial(add_kernel, at.start),
            in_specs=[VMEM] * (2 + len(more)),
            out_specs=VMEM,
            out_shape=jax.ShapeDtypeStruct(block.shape, jnp.bfloat16),
            compiler_params=params(),
            cost_estimate=cost,
            name="add_%d" % p,
        )(kept[p], block, *more)

    whole, halves = slice(0, PAIRS), [slice(0, PAIRS // 2), slice(PAIRS // 2, PAIRS)]
    pieces = {p: halves if p < 3 else [whole] for p in range(1, count)}
    cuts = [(t, at) for t, (p, mine) in enumerate(plan[1]) for at in ([whole] if mine else pieces[p])]
    came = {0: [across(sent)]}
    outs = pl.pallas_call(
        functools.partial(next_kernel, elems, 1, cuts),
        in_specs=[SMEM] * 3 + [VMEM] * 3,
        out_specs=[VMEM] * len(cuts),
        out_shape=[
            jax.ShapeDtypeStruct((at.stop - at.start, half, 2 * B), jnp.float32 if plan[1][t][1] else jnp.bfloat16)
            for t, at in cuts
        ],
        scratch_shapes=[pltpu.VMEM((1 + len(plan[1]) * PAIRS, half, 2 * B), jnp.float32)],
        compiler_params=params(),
        cost_estimate=long,
        name="next",
    )(codes, lists, counts, rows, near, weights)
    kept = outs[-count:]
    first = summed(0, whole, came[0][0])
    sent = outs[:-count]
    straight = along(first, [(1, 2), (2, 1)])
    joined = along(first, [(0, 1), (3, 2)])
    came[1] = [across(sent[0]), across(behind(sent[1], first))]
    ready1 = [summed(1, at, block) for at, block in zip(halves, came[1])]
    round1 = [along(block, ROUNDS[0]) for block in ready1]
    came[2] = [across(behind(sent[2], came[1][0])), across(behind(sent[3], came[1][1], straight, joined))]
    came[2][1] = behind(came[2][1], *round1)
    came[2][0] = behind(came[2][0], round1[0])
    ready2 = [summed(2, at, block, joined) for at, block in zip(halves, came[2])]
    round2 = [along(block, ROUNDS[1]) for block in ready2]
    came[3] = [across(behind(sent[4], came[2][0]))]

    total = pl.pallas_call(
        gather_kernel,
        in_specs=[VMEM] * 4,
        out_specs=VMEM,
        out_shape=jax.ShapeDtypeStruct(table, jnp.float32),
        compiler_params=params(),
        cost_estimate=pl.CostEstimate(flops=1_000_000_000, bytes_accessed=1000, transcendentals=0),
        name="gather",
    )(kept[count - 1], straight, *round1)
    parts = round2 + came[count - 1]
    coarse = pl.pallas_call(
        last_kernel,
        in_specs=[VMEM] * (1 + len(parts)),
        out_specs=VMEM,
        out_shape=jax.ShapeDtypeStruct((AGG_DEV, half, CS * CB), jnp.float32),
        scratch_shapes=[pltpu.VMEM(table, jnp.float32)],
        compiler_params=params(),
        cost_estimate=cost,
        name="last",
    )(total, *parts)
    return coarse.transpose(1, 0, 2)


def direct(jacobian, prolong, face_pattern, owner, member, coarse_slot):
    elems = jacobian.shape[0]
    owners = lax.axis_size(("elem", "sub"))
    capacity = max(2, 2 * elems // owners)
    device = lax.axis_index(("elem", "sub"))
    half = prolong.shape[0]
    rim = elems // 4
    before, after = halo(prolong, rim * B)
    ghosts = jnp.concatenate([before, prolong, after], axis=1).reshape(half, elems + 2 * rim, B)
    whole = lax.all_gather(prolong, "col", axis=0, tiled=True).reshape(CB, elems, B)
    first_row = device * elems - rim
    selfcol = jnp.arange(elems, dtype=jnp.int32)[:, None] + rim
    remote = jnp.where(face_pattern >= 0, face_pattern - first_row, 0)
    columns = jnp.concatenate([selfcol, remote], axis=1)
    present = jnp.concatenate([jnp.ones((elems, 1), jnp.bool_), face_pattern >= 0], axis=1)
    neighbour_rows = ghosts[:, columns, :] * present[None, :, :, None].astype(jnp.bfloat16)
    blocks = jacobian.reshape(elems, FACES + 1, B, B)
    product = jnp.einsum(
        "ejik,cejk->ejic", blocks, neighbour_rows, preferred_element_type=jnp.float32
    ).astype(jnp.bfloat16)
    owner_flat = owner[:, 0]
    marks = (owner_flat[:, None] == jnp.arange(owners, dtype=jnp.int32)[None, :]).astype(jnp.int32)
    ranking = jnp.sum(jnp.cumsum(marks, axis=0) * marks, axis=1) - 1
    place = owner_flat * capacity + ranking
    target = member[:, None] * CS + coarse_slot
    slots = owners * capacity
    labels = jnp.full((slots, FACES + 1), -1, jnp.int32).at[place].set(target)
    contribution = jnp.einsum("rei,ejic->ejcr", whole, product, preferred_element_type=jnp.float32)
    payload = jnp.zeros((slots, FACES + 1, half, CB), jnp.float32).at[place].set(contribution)
    axes = ("elem", "sub")
    arrived = lax.all_to_all(payload, axes, split_axis=0, concat_axis=0, tiled=True)
    arrived_labels = lax.all_to_all(labels, axes, split_axis=0, concat_axis=0, tiled=True)
    items = slots * (FACES + 1)
    values = arrived.reshape(items, half * CB)
    flat_labels = arrived_labels.reshape(items)
    destination = jnp.where(flat_labels >= 0, flat_labels, BLOCKS).astype(jnp.int32)
    summed = jnp.zeros((BLOCKS, half * CB), jnp.float32).at[destination].add(values, mode="drop")
    summed = summed.reshape(AGG_DEV, CS, half, CB).transpose(2, 0, 1, 3)
    return summed.reshape(half, AGG_DEV, CS * CB)


def shards(jacobian, *rest):
    elems = jacobian.shape[0]
    owners = lax.axis_size(("elem", "sub"))
    capacity = max(2, 2 * elems // owners)
    if lax.axis_size("sub") == 2 and lax.axis_size("elem") == 4 and BLOCKS <= capacity * (FACES + 1):
        return dense(jacobian, *rest)
    return direct(jacobian, *rest)


def solution(mesh):
    in_specs = (
        P(("groups", "elem", "sub"), None),
        P("col", ("groups", "elem", "sub")),
        P(("groups", "elem", "sub"), None),
        P(("groups", "elem", "sub"), None),
        P(("groups", "elem", "sub")),
        P(("groups", "elem", "sub"), None),
    )
    out_specs = P("col", ("groups", "elem", "sub"), None)
    return jax.shard_map(shards, mesh=mesh, in_specs=in_specs, out_specs=out_specs, check_vma=False)
```

```python
import functools

import jax
import jax.numpy as jnp
from jax import lax
from jax.experimental import pallas as pl
from jax.experimental.pallas import tpu as pltpu
from jax.sharding import PartitionSpec as P

B = 64
CB = 64
FACES = 4
CS = 9
AGG_DEV = 12
BLOCKS = AGG_DEV * CS
PAIRS = BLOCKS // 2
STEP = 16
UNROLL = 8
VMEM = pl.BlockSpec(memory_space=pltpu.VMEM)
SMEM = pl.BlockSpec(memory_space=pltpu.SMEM)
NT = (((1,), (1,)), ((), ()))


def params(mib=16):
    return pltpu.CompilerParams(vmem_limit_bytes=mib * 1024 * 1024)


def halo(cells, width):
    axes = ("elem", "sub")
    count = lax.axis_size(axes)
    up = [(i, i + 1) for i in range(count - 1)]
    down = [(i + 1, i) for i in range(count - 1)]
    return (
        lax.ppermute(cells[:, -width:], axes, up),
        lax.ppermute(cells[:, :width], axes, down),
    )


def halo_swaps(cells, width):
    axes = ("elem", "sub")
    count = lax.axis_size(axes)
    even = lax.axis_index(axes) % 2 == 0
    tail, head = cells[:, -width:], cells[:, :width]

    def swap(block, first):
        pairs = [(i, i + 1) for i in range(first, count - 1, 2)]
        return lax.ppermute(block, axes, pairs + [(j, i) for i, j in pairs])

    return swap(jnp.where(even, tail, head), 0), swap(jnp.where(even, head, tail), 1)


MEMBER, SLOT, FACE = 1, 2, 3 + FACES
CELL, TARGET = 0, FACES
LANES = 128


ROUNDS = ([(0, 2), (1, 0), (2, 3), (3, 1)], [(0, 1), (1, 3), (2, 0), (3, 2)])


def place_of(z, dest):
    if dest in (z, z ^ 3):
        return 3 if dest == z else 0
    return 1 if (z, dest) in ROUNDS[0] else 2


def call_plan(count):
    sent = [(p, 0) for p in range(count)]
    kept = [(p, 1) for p in range(count)]
    return [sent[:1], sent[1:] + kept]


def lists_kernel(elems, count, ints_ref, again_ref, code_ref, list_ref, count_ref):
    me = lax.axis_index("sub")
    z = lax.axis_index("elem")
    plan = call_plan(count)
    code = {table: (c, t) for c, tables in enumerate(plan) for t, table in enumerate(tables)}
    numbers, calls = 0, 0
    for d in range(count):
        for x in range(2):
            values = [0, 0]
            for y in range(count):
                for mine in range(2):
                    here = (z == y) & ((me == x) if mine else (me != x))
                    for i in range(2):
                        values[i] = jnp.where(here, code[place_of(y, d), mine][i], values[i])
            calls += values[0] << (2 * d + x)
            numbers += values[1] << (3 * (2 * d + x))

    device = z * lax.axis_size("sub") + me
    rim = elems // 4
    faces = again_ref[FACE:FACE + FACES, :]
    code_ref[...] = jnp.zeros_like(code_ref)
    code_ref[CELL:CELL + FACES, :elems] = jnp.where(faces >= 0, faces - (device * elems - rim), elems + 2 * rim)
    code_ref[TARGET:TARGET + FACES + 1, :elems] = (
        again_ref[MEMBER:MEMBER + 1, :] * CS + again_ref[SLOT:SLOT + FACES + 1, :])

    zero, one = 0, 0
    for start in range(0, elems, STEP):
        owners = [ints_ref[0, e] for e in range(start, start + STEP)]
        for e, owner in zip(range(start, start + STEP), owners):
            call = (calls >> owner) & 1
            number = (numbers >> (3 * owner)) & 7
            list_ref[call, jnp.where(call == 0, zero, one)] = LANES * BLOCKS * number + (2 * LANES + e)
            zero, one = zero + 1 - call, one + call
    for call, number in enumerate((zero, one)):
        count_ref[call] = number
        for u in range(UNROLL):
            list_ref[call, number + u] = elems


def near_kernel(cells_ref, other_ref, after_ref, near_ref, weight_ref):
    near_blocks(near_ref, 0, cells_ref)
    own_weights(weight_ref, cells_ref, other_ref)


def rows_kernel(jac_ref, after_ref, rows_ref):
    width = 2048

    def step(i, carry):
        at = pl.ds(pl.multiple_of(i * STEP, STEP), STEP)
        for q in range(jac_ref.shape[1] // width):
            part = jac_ref[at, q * width:(q + 1) * width]
            rows_ref[at, q * 16:(q + 1) * 16] = pltpu.einshape("a(bc)->abc", part, b=16, c=128)
        return carry

    lax.fori_loop(0, jac_ref.shape[0] // STEP, step, 0)


def accumulate(call, elems, code_ref, list_ref, count_ref, rows_ref, near_ref, weight_ref, total):
    low = lax.broadcasted_iota(jnp.int32, (32, 128), 1) < B
    high = jnp.where(low, 0, 1)
    total[...] = jnp.zeros_like(total)

    def body(it, carry):
        items = []
        for u in range(UNROLL):
            entry = list_ref[call, it * UNROLL + u]
            at = entry & (LANES - 1)
            items.append((at, jnp.minimum(at, elems - 1), entry >> 7))
        products = []
        for at, e, base in items:
            parts = []
            for j in range(FACES + 1):
                cell = near_ref[e + elems // 4 if j == 0 else code_ref[CELL + j - 1, at]]
                zero = jnp.zeros_like(cell)
                both = jnp.concatenate([jnp.where(low, cell, zero), jnp.where(low, zero, cell)], axis=0)
                block = rows_ref[e, j * 32:(j + 1) * 32, :]
                part = lax.dot_general(both, block, NT, preferred_element_type=jnp.float32)
                parts.append(jnp.concatenate([part[:32], part[32:]], axis=1))
            products.append(jnp.concatenate(parts, axis=0).astype(jnp.bfloat16))
        results = []
        for (at, e, base), product in zip(items, products):
            own = weight_ref[e]
            own = jnp.concatenate([own, own], axis=0)
            results.append(lax.dot_general(product, own, NT, preferred_element_type=jnp.float32))
        for (at, e, base), result in zip(items, results):
            for j in range(FACES + 1):
                target = base + code_ref[TARGET + j, at]
                part = result[j * 32:(j + 1) * 32, :]
                total[target >> 1] += jnp.where(high == (target & 1), part, 0.0)
        return carry

    lax.fori_loop(0, (count_ref[call] + UNROLL - 1) // UNROLL, body, 0)


def near_blocks(near_ref, base, cells_ref):
    low = lax.broadcasted_iota(jnp.int32, (32, 128), 1) < B
    for p in range(cells_ref.shape[1] // 128):
        pair = cells_ref[:, p * 128:(p + 1) * 128].astype(jnp.float32)
        turned = pltpu.roll(pair, B, 1)
        near_ref[base + 2 * p] = jnp.where(low, pair, turned).astype(jnp.bfloat16)
        near_ref[base + 2 * p + 1] = jnp.where(low, turned, pair).astype(jnp.bfloat16)


def own_weights(weight_ref, cells_ref, other_ref):
    row = lax.broadcasted_iota(jnp.int32, (128, 128), 0)
    col = lax.broadcasted_iota(jnp.int32, (128, 128), 1)
    source = (col // B) * B + 2 * (col % 32) + (col % B) // 32
    pick = jnp.where(row == source, 1.0, 0.0).astype(jnp.bfloat16)
    low_first = lax.axis_index("col") == 0
    step = 8
    for p in range(0, cells_ref.shape[1] // 128, step):
        stacked = []
        for q in range(p, p + step):
            own, other = cells_ref[:, q * 128:(q + 1) * 128], other_ref[:, q * 128:(q + 1) * 128]
            stacked += [jnp.where(low_first, own, other), jnp.where(low_first, other, own)]
        moved = jnp.dot(jnp.concatenate(stacked, axis=0), pick, preferred_element_type=jnp.float32)
        for q in range(step):
            pair = moved[q * CB:(q + 1) * CB]
            for h in range(2):
                weight_ref[2 * (p + q) + h] = pair[:, h * B:(h + 1) * B].astype(jnp.bfloat16)


def first_kernel(elems, code_ref, list_ref, count_ref, rows_ref, own_ref, weight_ref, one_ref, two_ref, *rest):
    outs, near_ref, total = rest[:-2], rest[-2], rest[-1]
    rim = elems // 4
    device = lax.axis_index("elem") * lax.axis_size("sub") + lax.axis_index("sub")
    even = device % 2 == 0
    near_ref[rim:rim + elems] = own_ref[...]
    near_blocks(near_ref, jnp.where(even, rim + elems, 0), one_ref)
    near_blocks(near_ref, jnp.where(even, 0, rim + elems), two_ref)
    near_ref[near_ref.shape[0] - 1] = jnp.zeros((32, 128), jnp.bfloat16)
    accumulate(0, elems, code_ref, list_ref, count_ref, rows_ref, near_ref, weight_ref, total)
    for k, out in enumerate(outs):
        out[...] = total[1 + k * PAIRS // 2:1 + (k + 1) * PAIRS // 2].astype(out.dtype)


def next_kernel(elems, call, cuts, code_ref, list_ref, count_ref, rows_ref, near_ref, weight_ref, *rest):
    outs, total = rest[:-1], rest[-1]
    accumulate(call, elems, code_ref, list_ref, count_ref, rows_ref, near_ref, weight_ref, total)
    for (t, at), out in zip(cuts, outs):
        start = 1 + t * PAIRS
        out[...] = total[start + at.start:start + at.stop].astype(out.dtype)


def add_kernel(start, joins, kept_ref, came_ref, *rest):
    out_ref = rest[-1]
    value = kept_ref[start:start + out_ref.shape[0]] + came_ref[...].astype(jnp.float32)
    if joins is not None:
        outer = (lax.axis_index("elem") + 1) % 4 < 2
        value = value + jnp.where(outer == joins, rest[0][...].astype(jnp.float32), 0.0)
    out_ref[...] = value.astype(out_ref.dtype)


def gather_kernel(own_ref, *rest):
    parts, total = rest[:-1], rest[-1]
    total[...] = own_ref[...]
    at = 0
    for part in parts:
        total[at:at + part.shape[0]] += part[...].astype(jnp.float32)
        at = (at + part.shape[0]) % PAIRS


def last_kernel(*rest):
    out_ref, total = rest[-2], rest[-1]
    gather_kernel(*rest[:-2], total)
    low = lax.broadcasted_iota(jnp.int32, (32, 128), 1) < B
    for a in range(AGG_DEV):
        first = a * CS // 2
        for q in range(CS // 2):
            if a % 2 == 0:
                out_ref[a, :, q * 128:(q + 1) * 128] = total[first + q]
            else:
                out_ref[a, :, q * 128:(q + 1) * 128] = jnp.where(
                    low, pltpu.roll(total[first + q], B, 1), pltpu.roll(total[first + q + 1], B, 1))
        last = total[first + CS // 2]
        if a % 2 == 1:
            last = pltpu.roll(last, B, 1)
        out_ref[a, :, (CS // 2) * 128:] = last[:, :B]


def dense(jacobian, prolong, face_pattern, owner, member, coarse_slot):
    elems = jacobian.shape[0]
    half = prolong.shape[0]
    count = lax.axis_size("elem")
    rim = elems // 4
    tiles = jacobian.shape[1] // 128
    plan = call_plan(count)
    cost = pl.CostEstimate(flops=1000, bytes_accessed=1000, transcendentals=0)

    other = lax.ppermute(prolong, "col", [(0, 1), (1, 0)])
    one, two = halo_swaps(prolong, rim * B)
    ints = jnp.concatenate([owner.T, member[None], coarse_slot.T, face_pattern.T], axis=0)

    long = pl.CostEstimate(flops=20_000_000_000, bytes_accessed=1000, transcendentals=0)
    codes, lists, counts = pl.pallas_call(
        functools.partial(lists_kernel, elems, count),
        in_specs=[SMEM, VMEM],
        out_specs=[VMEM, SMEM, SMEM],
        out_shape=[
            jax.ShapeDtypeStruct((16, LANES), jnp.int32),
            jax.ShapeDtypeStruct((len(plan), elems + UNROLL), jnp.int32),
            jax.ShapeDtypeStruct((len(plan),), jnp.int32),
        ],
        compiler_params=params(),
        cost_estimate=long,
        name="lists",
    )(ints, ints)
    own_near, weights = pl.pallas_call(
        near_kernel,
        in_specs=[VMEM, VMEM, pl.BlockSpec(memory_space=pl.ANY)],
        out_specs=[VMEM, VMEM],
        out_shape=[
            jax.ShapeDtypeStruct((elems, half, 2 * B), jnp.bfloat16),
            jax.ShapeDtypeStruct((elems, CB, B), jnp.bfloat16),
        ],
        compiler_params=params(),
        cost_estimate=cost,
        name="near",
    )(prolong, other, codes)
    rows = pl.pallas_call(
        rows_kernel,
        in_specs=[VMEM, pl.BlockSpec(memory_space=pl.ANY)],
        out_specs=VMEM,
        out_shape=jax.ShapeDtypeStruct((elems, tiles, 128), jnp.bfloat16),
        compiler_params=params(),
        cost_estimate=cost,
        name="rows",
    )(jacobian, own_near)

    table = (PAIRS, half, 2 * B)
    *sent, near = pl.pallas_call(
        functools.partial(first_kernel, elems),
        in_specs=[SMEM] * 3 + [VMEM] * 5,
        out_specs=[VMEM] * 3,
        out_shape=[jax.ShapeDtypeStruct((PAIRS // 2, half, 2 * B), jnp.bfloat16)] * 2 + [
            jax.ShapeDtypeStruct((elems + 2 * rim + 1, half, 2 * B), jnp.bfloat16),
        ],
        scratch_shapes=[pltpu.VMEM((1 + PAIRS, half, 2 * B), jnp.float32)],
        compiler_params=params(),
        cost_estimate=cost,
        name="first",
    )(codes, lists, counts, rows, own_near, weights, one, two)

    def across(block):
        return lax.ppermute(block, "sub", [(0, 1), (1, 0)])

    def along(block, pairs):
        return lax.ppermute(block, "elem", pairs)

    def behind(block, *others):
        return lax.optimization_barrier((block, *others))[0]

    def summed(p, at, block, joins=None, *more):
        return pl.pallas_call(
            functools.partial(add_kernel, at.start, joins),
            in_specs=[VMEM] * (2 + len(more)),
            out_specs=VMEM,
            out_shape=jax.ShapeDtypeStruct(block.shape, jnp.bfloat16),
            compiler_params=params(),
            cost_estimate=cost,
            name="add_%d" % p,
        )(kept[p], block, *more)

    whole, halves = slice(0, PAIRS), [slice(0, PAIRS // 2), slice(PAIRS // 2, PAIRS)]
    pieces = {p: halves if p < 3 else [whole] for p in range(1, count)}
    cuts = [(t, at) for t, (p, mine) in enumerate(plan[1]) for at in ([whole] if mine else pieces[p])]
    came = {0: [across(block) for block in sent]}
    outs = pl.pallas_call(
        functools.partial(next_kernel, elems, 1, cuts),
        in_specs=[SMEM] * 3 + [VMEM] * 3,
        out_specs=[VMEM] * len(cuts),
        out_shape=[
            jax.ShapeDtypeStruct((at.stop - at.start, half, 2 * B), jnp.float32 if plan[1][t][1] else jnp.bfloat16)
            for t, at in cuts
        ],
        scratch_shapes=[pltpu.VMEM((1 + len(plan[1]) * PAIRS, half, 2 * B), jnp.float32)],
        compiler_params=params(),
        cost_estimate=long,
        name="next",
    )(codes, lists, counts, rows, near, weights)
    kept = outs[-count:]
    sent = outs[:-count]
    ready0 = [summed(0, at, block) for at, block in zip(halves, came[0])]
    joined = [along(block, [(y, y ^ 1) for y in range(count)]) for block in ready0]
    came[1] = [across(sent[0]), across(behind(sent[1], came[0][1]))]
    ready1 = [summed(1, at, block, True, more) for at, block, more in zip(halves, came[1], joined)]
    round1 = [along(block, ROUNDS[0]) for block in ready1]
    came[2] = [across(behind(sent[2], joined[0])), across(behind(sent[3], came[1][1]))]
    came[2][0] = behind(came[2][0], round1[0])
    came[2][1] = behind(came[2][1], *round1)
    ready2 = [summed(2, at, block, False, more) for at, block, more in zip(halves, came[2], joined)]
    round2 = [along(block, ROUNDS[1]) for block in ready2]
    came[3] = [across(behind(sent[4], came[2][0]))]

    total = pl.pallas_call(
        gather_kernel,
        in_specs=[VMEM] * 3,
        out_specs=VMEM,
        out_shape=jax.ShapeDtypeStruct(table, jnp.float32),
        compiler_params=params(),
        cost_estimate=pl.CostEstimate(flops=1_000_000_000, bytes_accessed=1000, transcendentals=0),
        name="gather",
    )(kept[count - 1], *round1)
    parts = round2 + came[count - 1]
    coarse = pl.pallas_call(
        last_kernel,
        in_specs=[VMEM] * (1 + len(parts)),
        out_specs=VMEM,
        out_shape=jax.ShapeDtypeStruct((AGG_DEV, half, CS * CB), jnp.float32),
        scratch_shapes=[pltpu.VMEM(table, jnp.float32)],
        compiler_params=params(),
        cost_estimate=cost,
        name="last",
    )(total, *parts)
    return coarse.transpose(1, 0, 2)


def direct(jacobian, prolong, face_pattern, owner, member, coarse_slot):
    elems = jacobian.shape[0]
    owners = lax.axis_size(("elem", "sub"))
    capacity = max(2, 2 * elems // owners)
    device = lax.axis_index(("elem", "sub"))
    half = prolong.shape[0]
    rim = elems // 4
    before, after = halo(prolong, rim * B)
    ghosts = jnp.concatenate([before, prolong, after], axis=1).reshape(half, elems + 2 * rim, B)
    whole = lax.all_gather(prolong, "col", axis=0, tiled=True).reshape(CB, elems, B)
    first_row = device * elems - rim
    selfcol = jnp.arange(elems, dtype=jnp.int32)[:, None] + rim
    remote = jnp.where(face_pattern >= 0, face_pattern - first_row, 0)
    columns = jnp.concatenate([selfcol, remote], axis=1)
    present = jnp.concatenate([jnp.ones((elems, 1), jnp.bool_), face_pattern >= 0], axis=1)
    neighbour_rows = ghosts[:, columns, :] * present[None, :, :, None].astype(jnp.bfloat16)
    blocks = jacobian.reshape(elems, FACES + 1, B, B)
    product = jnp.einsum(
        "ejik,cejk->ejic", blocks, neighbour_rows, preferred_element_type=jnp.float32
    ).astype(jnp.bfloat16)
    owner_flat = owner[:, 0]
    marks = (owner_flat[:, None] == jnp.arange(owners, dtype=jnp.int32)[None, :]).astype(jnp.int32)
    ranking = jnp.sum(jnp.cumsum(marks, axis=0) * marks, axis=1) - 1
    place = owner_flat * capacity + ranking
    target = member[:, None] * CS + coarse_slot
    slots = owners * capacity
    labels = jnp.full((slots, FACES + 1), -1, jnp.int32).at[place].set(target)
    contribution = jnp.einsum("rei,ejic->ejcr", whole, product, preferred_element_type=jnp.float32)
    payload = jnp.zeros((slots, FACES + 1, half, CB), jnp.float32).at[place].set(contribution)
    axes = ("elem", "sub")
    arrived = lax.all_to_all(payload, axes, split_axis=0, concat_axis=0, tiled=True)
    arrived_labels = lax.all_to_all(labels, axes, split_axis=0, concat_axis=0, tiled=True)
    items = slots * (FACES + 1)
    values = arrived.reshape(items, half * CB)
    flat_labels = arrived_labels.reshape(items)
    destination = jnp.where(flat_labels >= 0, flat_labels, BLOCKS).astype(jnp.int32)
    summed = jnp.zeros((BLOCKS, half * CB), jnp.float32).at[destination].add(values, mode="drop")
    summed = summed.reshape(AGG_DEV, CS, half, CB).transpose(2, 0, 1, 3)
    return summed.reshape(half, AGG_DEV, CS * CB)


def shards(jacobian, *rest):
    elems = jacobian.shape[0]
    owners = lax.axis_size(("elem", "sub"))
    capacity = max(2, 2 * elems // owners)
    if lax.axis_size("sub") == 2 and lax.axis_size("elem") == 4 and BLOCKS <= capacity * (FACES + 1):
        return dense(jacobian, *rest)
    return direct(jacobian, *rest)


def solution(mesh):
    in_specs = (
        P(("groups", "elem", "sub"), None),
        P("col", ("groups", "elem", "sub")),
        P(("groups", "elem", "sub"), None),
        P(("groups", "elem", "sub"), None),
        P(("groups", "elem", "sub")),
        P(("groups", "elem", "sub"), None),
    )
    out_specs = P("col", ("groups", "elem", "sub"), None)
    return jax.shard_map(shards, mesh=mesh, in_specs=in_specs, out_specs=out_specs, check_vma=False)
```

```python
import functools

import jax
import jax.numpy as jnp
from jax import lax
from jax.experimental import pallas as pl
from jax.experimental.pallas import tpu as pltpu
from jax.sharding import PartitionSpec as P

B = 64
CB = 64
FACES = 4
CS = 9
AGG_DEV = 12
BLOCKS = AGG_DEV * CS
PAIRS = BLOCKS // 2
STEP = 16
UNROLL = 8
VMEM = pl.BlockSpec(memory_space=pltpu.VMEM)
SMEM = pl.BlockSpec(memory_space=pltpu.SMEM)
NT = (((1,), (1,)), ((), ()))


def params(mib=16):
    return pltpu.CompilerParams(vmem_limit_bytes=mib * 1024 * 1024)


def halo(cells, width):
    axes = ("elem", "sub")
    count = lax.axis_size(axes)
    up = [(i, i + 1) for i in range(count - 1)]
    down = [(i + 1, i) for i in range(count - 1)]
    return (
        lax.ppermute(cells[:, -width:], axes, up),
        lax.ppermute(cells[:, :width], axes, down),
    )


def halo_swaps(cells, width):
    axes = ("elem", "sub")
    count = lax.axis_size(axes)
    even = lax.axis_index(axes) % 2 == 0
    tail, head = cells[:, -width:], cells[:, :width]

    def swap(block, first):
        pairs = [(i, i + 1) for i in range(first, count - 1, 2)]
        return lax.ppermute(block, axes, pairs + [(j, i) for i, j in pairs])

    return swap(jnp.where(even, tail, head), 0), swap(jnp.where(even, head, tail), 1)


MEMBER, SLOT, FACE = 1, 2, 3 + FACES
CELL, TARGET = 0, FACES
LANES = 128


ROUNDS = ([(0, 2), (1, 0), (2, 3), (3, 1)], [(0, 1), (1, 3), (2, 0), (3, 2)])


def place_of(z, dest):
    if dest in (z, z ^ 3):
        return 3 if dest == z else 0
    return 1 if (z, dest) in ROUNDS[0] else 2


def call_plan(count):
    sent = [(p, 0) for p in range(count)]
    kept = [(p, 1) for p in range(count)]
    return [sent[:1], [sent[1], kept[0]], [sent[2], kept[1]], [sent[3], kept[2], kept[3]]]


def lists_kernel(elems, count, ints_ref, again_ref, code_ref, list_ref, count_ref):
    me = lax.axis_index("sub")
    z = lax.axis_index("elem")
    plan = call_plan(count)
    code = {table: (c, t) for c, tables in enumerate(plan) for t, table in enumerate(tables)}
    numbers, calls = 0, 0
    for d in range(count):
        for x in range(2):
            values = [0, 0]
            for y in range(count):
                for mine in range(2):
                    here = (z == y) & ((me == x) if mine else (me != x))
                    for i in range(2):
                        values[i] = jnp.where(here, code[place_of(y, d), mine][i], values[i])
            calls += values[0] << (2 * (2 * d + x))
            numbers += values[1] << (3 * (2 * d + x))

    device = z * lax.axis_size("sub") + me
    rim = elems // 4
    faces = again_ref[FACE:FACE + FACES, :]
    code_ref[...] = jnp.zeros_like(code_ref)
    code_ref[CELL:CELL + FACES, :elems] = jnp.where(faces >= 0, faces - (device * elems - rim), elems + 2 * rim)
    code_ref[TARGET:TARGET + FACES + 1, :elems] = (
        again_ref[MEMBER:MEMBER + 1, :] * CS + again_ref[SLOT:SLOT + FACES + 1, :])

    lengths = 0
    for start in range(0, elems, STEP):
        owners = [ints_ref[0, e] for e in range(start, start + STEP)]
        for e, owner in zip(range(start, start + STEP), owners):
            call = (calls >> (2 * owner)) & 3
            number = (numbers >> (3 * owner)) & 7
            list_ref[call, (lengths >> (8 * call)) & 127] = LANES * BLOCKS * number + (2 * LANES + e)
            lengths += 1 << (8 * call)
    for call in range(len(plan)):
        length = (lengths >> (8 * call)) & 127
        count_ref[call] = length
        for u in range(UNROLL):
            list_ref[call, length + u] = elems


def near_kernel(cells_ref, other_ref, after_ref, near_ref, weight_ref):
    near_blocks(near_ref, 0, cells_ref)
    own_weights(weight_ref, cells_ref, other_ref)


def rows_kernel(jac_ref, after_ref, rows_ref):
    width = 2048

    def step(i, carry):
        at = pl.ds(pl.multiple_of(i * STEP, STEP), STEP)
        for q in range(jac_ref.shape[1] // width):
            part = jac_ref[at, q * width:(q + 1) * width]
            rows_ref[at, q * 16:(q + 1) * 16] = pltpu.einshape("a(bc)->abc", part, b=16, c=128)
        return carry

    lax.fori_loop(0, jac_ref.shape[0] // STEP, step, 0)


def accumulate(call, elems, code_ref, list_ref, count_ref, rows_ref, near_ref, weight_ref, total):
    low = lax.broadcasted_iota(jnp.int32, (32, 128), 1) < B
    high = jnp.where(low, 0, 1)
    total[...] = jnp.zeros_like(total)

    def body(it, carry):
        items = []
        for u in range(UNROLL):
            entry = list_ref[call, it * UNROLL + u]
            at = entry & (LANES - 1)
            items.append((at, jnp.minimum(at, elems - 1), entry >> 7))
        products = []
        for at, e, base in items:
            parts = []
            for j in range(FACES + 1):
                cell = near_ref[e + elems // 4 if j == 0 else code_ref[CELL + j - 1, at]]
                zero = jnp.zeros_like(cell)
                both = jnp.concatenate([jnp.where(low, cell, zero), jnp.where(low, zero, cell)], axis=0)
                block = rows_ref[e, j * 32:(j + 1) * 32, :]
                part = lax.dot_general(both, block, NT, preferred_element_type=jnp.float32)
                parts.append(jnp.concatenate([part[:32], part[32:]], axis=1))
            products.append(jnp.concatenate(parts, axis=0).astype(jnp.bfloat16))
        results = []
        for (at, e, base), product in zip(items, products):
            own = weight_ref[e]
            own = jnp.concatenate([own, own], axis=0)
            results.append(lax.dot_general(product, own, NT, preferred_element_type=jnp.float32))
        for (at, e, base), result in zip(items, results):
            for j in range(FACES + 1):
                target = base + code_ref[TARGET + j, at]
                part = result[j * 32:(j + 1) * 32, :]
                total[target >> 1] += jnp.where(high == (target & 1), part, 0.0)
        return carry

    lax.fori_loop(0, (count_ref[call] + UNROLL - 1) // UNROLL, body, 0)


def near_blocks(near_ref, base, cells_ref):
    low = lax.broadcasted_iota(jnp.int32, (32, 128), 1) < B
    for p in range(cells_ref.shape[1] // 128):
        pair = cells_ref[:, p * 128:(p + 1) * 128].astype(jnp.float32)
        turned = pltpu.roll(pair, B, 1)
        near_ref[base + 2 * p] = jnp.where(low, pair, turned).astype(jnp.bfloat16)
        near_ref[base + 2 * p + 1] = jnp.where(low, turned, pair).astype(jnp.bfloat16)


def own_weights(weight_ref, cells_ref, other_ref):
    row = lax.broadcasted_iota(jnp.int32, (128, 128), 0)
    col = lax.broadcasted_iota(jnp.int32, (128, 128), 1)
    source = (col // B) * B + 2 * (col % 32) + (col % B) // 32
    pick = jnp.where(row == source, 1.0, 0.0).astype(jnp.bfloat16)
    low_first = lax.axis_index("col") == 0
    step = 8
    for p in range(0, cells_ref.shape[1] // 128, step):
        stacked = []
        for q in range(p, p + step):
            own, other = cells_ref[:, q * 128:(q + 1) * 128], other_ref[:, q * 128:(q + 1) * 128]
            stacked += [jnp.where(low_first, own, other), jnp.where(low_first, other, own)]
        moved = jnp.dot(jnp.concatenate(stacked, axis=0), pick, preferred_element_type=jnp.float32)
        for q in range(step):
            pair = moved[q * CB:(q + 1) * CB]
            for h in range(2):
                weight_ref[2 * (p + q) + h] = pair[:, h * B:(h + 1) * B].astype(jnp.bfloat16)


def first_kernel(elems, code_ref, list_ref, count_ref, rows_ref, own_ref, weight_ref, two_ref, one_ref, *rest):
    outs, near_ref, total = rest[:-2], rest[-2], rest[-1]
    rim = elems // 4
    device = lax.axis_index("elem") * lax.axis_size("sub") + lax.axis_index("sub")
    even = device % 2 == 0
    near_ref[rim:rim + elems] = own_ref[...]
    near_blocks(near_ref, jnp.where(even, rim + elems, 0), one_ref)
    near_blocks(near_ref, jnp.where(even, 0, rim + elems), two_ref)
    near_ref[near_ref.shape[0] - 1] = jnp.zeros((32, 128), jnp.bfloat16)
    accumulate(0, elems, code_ref, list_ref, count_ref, rows_ref, near_ref, weight_ref, total)
    for k, out in enumerate(outs):
        out[...] = total[1 + k * PAIRS // 2:1 + (k + 1) * PAIRS // 2].astype(out.dtype)


def next_kernel(elems, call, cuts, code_ref, list_ref, count_ref, rows_ref, near_ref, weight_ref, after_ref, *rest):
    outs, total = rest[:-1], rest[-1]
    accumulate(call, elems, code_ref, list_ref, count_ref, rows_ref, near_ref, weight_ref, total)
    for (t, at), out in zip(cuts, outs):
        start = 1 + t * PAIRS
        out[...] = total[start + at.start:start + at.stop].astype(out.dtype)


def add_kernel(start, joins, kept_ref, came_ref, *rest):
    out_ref = rest[-1]
    value = kept_ref[start:start + out_ref.shape[0]] + came_ref[...].astype(jnp.float32)
    if joins is not None:
        outer = (lax.axis_index("elem") + 1) % 4 < 2
        value = value + jnp.where(outer == joins, rest[0][...].astype(jnp.float32), 0.0)
    out_ref[...] = value.astype(out_ref.dtype)


def gather_kernel(own_ref, *rest):
    parts, total = rest[:-1], rest[-1]
    total[...] = own_ref[...]
    at = 0
    for part in parts:
        total[at:at + part.shape[0]] += part[...].astype(jnp.float32)
        at = (at + part.shape[0]) % PAIRS


def last_kernel(*rest):
    out_ref, total = rest[-2], rest[-1]
    gather_kernel(*rest[:-2], total)
    low = lax.broadcasted_iota(jnp.int32, (32, 128), 1) < B
    for a in range(AGG_DEV):
        first = a * CS // 2
        for q in range(CS // 2):
            if a % 2 == 0:
                out_ref[a, :, q * 128:(q + 1) * 128] = total[first + q]
            else:
                out_ref[a, :, q * 128:(q + 1) * 128] = jnp.where(
                    low, pltpu.roll(total[first + q], B, 1), pltpu.roll(total[first + q + 1], B, 1))
        last = total[first + CS // 2]
        if a % 2 == 1:
            last = pltpu.roll(last, B, 1)
        out_ref[a, :, (CS // 2) * 128:] = last[:, :B]


def dense(jacobian, prolong, face_pattern, owner, member, coarse_slot):
    elems = jacobian.shape[0]
    half = prolong.shape[0]
    count = lax.axis_size("elem")
    rim = elems // 4
    tiles = jacobian.shape[1] // 128
    plan = call_plan(count)
    cost = pl.CostEstimate(flops=1000, bytes_accessed=1000, transcendentals=0)

    other = lax.ppermute(prolong, "col", [(0, 1), (1, 0)])
    one, two = halo_swaps(prolong, rim * B)
    ints = jnp.concatenate([owner.T, member[None], coarse_slot.T, face_pattern.T], axis=0)

    long = pl.CostEstimate(flops=20_000_000_000, bytes_accessed=1000, transcendentals=0)
    codes, lists, counts = pl.pallas_call(
        functools.partial(lists_kernel, elems, count),
        in_specs=[SMEM, VMEM],
        out_specs=[VMEM, SMEM, SMEM],
        out_shape=[
            jax.ShapeDtypeStruct((16, LANES), jnp.int32),
            jax.ShapeDtypeStruct((len(plan), elems + UNROLL), jnp.int32),
            jax.ShapeDtypeStruct((len(plan),), jnp.int32),
        ],
        compiler_params=params(),
        cost_estimate=long,
        name="lists",
    )(ints, ints)
    own_near, weights = pl.pallas_call(
        near_kernel,
        in_specs=[VMEM, VMEM, pl.BlockSpec(memory_space=pl.ANY)],
        out_specs=[VMEM, VMEM],
        out_shape=[
            jax.ShapeDtypeStruct((elems, half, 2 * B), jnp.bfloat16),
            jax.ShapeDtypeStruct((elems, CB, B), jnp.bfloat16),
        ],
        compiler_params=params(),
        cost_estimate=cost,
        name="near",
    )(prolong, other, codes)
    rows = pl.pallas_call(
        rows_kernel,
        in_specs=[VMEM, pl.BlockSpec(memory_space=pl.ANY)],
        out_specs=VMEM,
        out_shape=jax.ShapeDtypeStruct((elems, tiles, 128), jnp.bfloat16),
        compiler_params=params(),
        cost_estimate=cost,
        name="rows",
    )(jacobian, own_near)

    table = (PAIRS, half, 2 * B)
    *sent, near = pl.pallas_call(
        functools.partial(first_kernel, elems),
        in_specs=[SMEM] * 3 + [VMEM] * 5,
        out_specs=[VMEM] * 3,
        out_shape=[jax.ShapeDtypeStruct((PAIRS // 2, half, 2 * B), jnp.bfloat16)] * 2 + [
            jax.ShapeDtypeStruct((elems + 2 * rim + 1, half, 2 * B), jnp.bfloat16),
        ],
        scratch_shapes=[pltpu.VMEM((1 + PAIRS, half, 2 * B), jnp.float32)],
        compiler_params=params(),
        cost_estimate=cost,
        name="first",
    )(codes, lists, counts, rows, own_near, weights, two, one)

    def across(block):
        return lax.ppermute(block, "sub", [(0, 1), (1, 0)])

    def along(block, pairs):
        return lax.ppermute(block, "elem", pairs)

    def behind(block, *others):
        return lax.optimization_barrier((block, *others))[0]

    def summed(p, at, block, joins=None, *more):
        return pl.pallas_call(
            functools.partial(add_kernel, at.start, joins),
            in_specs=[VMEM] * (2 + len(more)),
            out_specs=VMEM,
            out_shape=jax.ShapeDtypeStruct(block.shape, jnp.bfloat16),
            compiler_params=params(),
            cost_estimate=cost,
            name="add_%d" % p,
        )(kept[p], block, *more)

    whole, halves = slice(0, PAIRS), [slice(0, PAIRS // 2), slice(PAIRS // 2, PAIRS)]
    pieces = {p: halves if p < 3 else [whole] for p in range(1, count)}
    def tables(call, after):
        cuts = [(t, at) for t, (p, mine) in enumerate(plan[call]) for at in ([whole] if mine else pieces[p])]
        outs = pl.pallas_call(
            functools.partial(next_kernel, elems, call, cuts),
            in_specs=[SMEM] * 3 + [VMEM] * 3 + [pl.BlockSpec(memory_space=pl.ANY)],
            out_specs=[VMEM] * len(cuts),
            out_shape=[
                jax.ShapeDtypeStruct(
                    (at.stop - at.start, half, 2 * B), jnp.float32 if plan[call][t][1] else jnp.bfloat16)
                for t, at in cuts
            ],
            scratch_shapes=[pltpu.VMEM((1 + len(plan[call]) * PAIRS, half, 2 * B), jnp.float32)],
            compiler_params=params(),
            cost_estimate=cost,
            name="tables_%d" % call,
        )(codes, lists, counts, rows, near, weights, after)
        for (t, at), out in zip(cuts, outs):
            p, mine = plan[call][t]
            if mine:
                kept[p] = out
            else:
                ready.setdefault(p, []).append(out)

    came = {0: [across(sent[0])]}
    kept, ready = {}, {}
    tables(1, near)
    came[0].append(across(sent[1]))
    ready0 = [summed(0, halves[0], came[0][0])]
    tables(2, ready0[0])
    came[0][1] = behind(came[0][1], ready0[0])
    ready0.append(summed(0, halves[1], came[0][1]))
    joined = [along(block, [(y, y ^ 1) for y in range(count)]) for block in ready0]
    tables(3, ready0[1])
    came[1] = [across(behind(ready[1][0], ready0[0])), across(behind(ready[1][1], came[0][1]))]
    ready1 = [summed(1, at, block, True, more) for at, block, more in zip(halves, came[1], joined)]
    round1 = [along(block, ROUNDS[0]) for block in ready1]
    came[2] = [across(behind(ready[2][0], joined[0]))]
    came[2].append(across(behind(ready[2][1], came[2][0])))
    came[2][0] = behind(came[2][0], round1[0])
    came[2][1] = behind(came[2][1], round1[0], round1[1])
    ready2 = [summed(2, at, block, False, more) for at, block, more in zip(halves, came[2], joined)]
    round2 = [along(block, ROUNDS[1]) for block in ready2]
    came[3] = [across(behind(ready[3][0], came[2][0]))]

    total = pl.pallas_call(
        gather_kernel,
        in_specs=[VMEM] * 3,
        out_specs=VMEM,
        out_shape=jax.ShapeDtypeStruct(table, jnp.float32),
        compiler_params=params(),
        cost_estimate=pl.CostEstimate(flops=1_000_000_000, bytes_accessed=1000, transcendentals=0),
        name="gather",
    )(kept[count - 1], *round1)
    parts = round2 + came[count - 1]
    coarse = pl.pallas_call(
        last_kernel,
        in_specs=[VMEM] * (1 + len(parts)),
        out_specs=VMEM,
        out_shape=jax.ShapeDtypeStruct((AGG_DEV, half, CS * CB), jnp.float32),
        scratch_shapes=[pltpu.VMEM(table, jnp.float32)],
        compiler_params=params(),
        cost_estimate=cost,
        name="last",
    )(total, *parts)
    return coarse.transpose(1, 0, 2)


def direct(jacobian, prolong, face_pattern, owner, member, coarse_slot):
    elems = jacobian.shape[0]
    owners = lax.axis_size(("elem", "sub"))
    capacity = max(2, 2 * elems // owners)
    device = lax.axis_index(("elem", "sub"))
    half = prolong.shape[0]
    rim = elems // 4
    before, after = halo(prolong, rim * B)
    ghosts = jnp.concatenate([before, prolong, after], axis=1).reshape(half, elems + 2 * rim, B)
    whole = lax.all_gather(prolong, "col", axis=0, tiled=True).reshape(CB, elems, B)
    first_row = device * elems - rim
    selfcol = jnp.arange(elems, dtype=jnp.int32)[:, None] + rim
    remote = jnp.where(face_pattern >= 0, face_pattern - first_row, 0)
    columns = jnp.concatenate([selfcol, remote], axis=1)
    present = jnp.concatenate([jnp.ones((elems, 1), jnp.bool_), face_pattern >= 0], axis=1)
    neighbour_rows = ghosts[:, columns, :] * present[None, :, :, None].astype(jnp.bfloat16)
    blocks = jacobian.reshape(elems, FACES + 1, B, B)
    product = jnp.einsum(
        "ejik,cejk->ejic", blocks, neighbour_rows, preferred_element_type=jnp.float32
    ).astype(jnp.bfloat16)
    owner_flat = owner[:, 0]
    marks = (owner_flat[:, None] == jnp.arange(owners, dtype=jnp.int32)[None, :]).astype(jnp.int32)
    ranking = jnp.sum(jnp.cumsum(marks, axis=0) * marks, axis=1) - 1
    place = owner_flat * capacity + ranking
    target = member[:, None] * CS + coarse_slot
    slots = owners * capacity
    labels = jnp.full((slots, FACES + 1), -1, jnp.int32).at[place].set(target)
    contribution = jnp.einsum("rei,ejic->ejcr", whole, product, preferred_element_type=jnp.float32)
    payload = jnp.zeros((slots, FACES + 1, half, CB), jnp.float32).at[place].set(contribution)
    axes = ("elem", "sub")
    arrived = lax.all_to_all(payload, axes, split_axis=0, concat_axis=0, tiled=True)
    arrived_labels = lax.all_to_all(labels, axes, split_axis=0, concat_axis=0, tiled=True)
    items = slots * (FACES + 1)
    values = arrived.reshape(items, half * CB)
    flat_labels = arrived_labels.reshape(items)
    destination = jnp.where(flat_labels >= 0, flat_labels, BLOCKS).astype(jnp.int32)
    summed = jnp.zeros((BLOCKS, half * CB), jnp.float32).at[destination].add(values, mode="drop")
    summed = summed.reshape(AGG_DEV, CS, half, CB).transpose(2, 0, 1, 3)
    return summed.reshape(half, AGG_DEV, CS * CB)


def shards(jacobian, *rest):
    elems = jacobian.shape[0]
    owners = lax.axis_size(("elem", "sub"))
    capacity = max(2, 2 * elems // owners)
    if lax.axis_size("sub") == 2 and lax.axis_size("elem") == 4 and BLOCKS <= capacity * (FACES + 1):
        return dense(jacobian, *rest)
    return direct(jacobian, *rest)


def solution(mesh):
    in_specs = (
        P(("groups", "elem", "sub"), None),
        P("col", ("groups", "elem", "sub")),
        P(("groups", "elem", "sub"), None),
        P(("groups", "elem", "sub"), None),
        P(("groups", "elem", "sub")),
        P(("groups", "elem", "sub"), None),
    )
    out_specs = P("col", ("groups", "elem", "sub"), None)
    return jax.shard_map(shards, mesh=mesh, in_specs=in_specs, out_specs=out_specs, check_vma=False)
```

```python
import functools

import jax
import jax.numpy as jnp
from jax import lax
from jax.experimental import pallas as pl
from jax.experimental.pallas import tpu as pltpu
from jax.sharding import PartitionSpec as P

B = 64
CB = 64
FACES = 4
CS = 9
AGG_DEV = 12
BLOCKS = AGG_DEV * CS
PAIRS = BLOCKS // 2
STEP = 16
UNROLL = 8
VMEM = pl.BlockSpec(memory_space=pltpu.VMEM)
SMEM = pl.BlockSpec(memory_space=pltpu.SMEM)
NT = (((1,), (1,)), ((), ()))


def params(mib=16):
    return pltpu.CompilerParams(vmem_limit_bytes=mib * 1024 * 1024)


def halo(cells, width):
    axes = ("elem", "sub")
    count = lax.axis_size(axes)
    up = [(i, i + 1) for i in range(count - 1)]
    down = [(i + 1, i) for i in range(count - 1)]
    return (
        lax.ppermute(cells[:, -width:], axes, up),
        lax.ppermute(cells[:, :width], axes, down),
    )


def halo_swaps(cells, width):
    axes = ("elem", "sub")
    count = lax.axis_size(axes)
    even = lax.axis_index(axes) % 2 == 0
    tail, head = cells[:, -width:], cells[:, :width]

    def swap(block, first):
        pairs = [(i, i + 1) for i in range(first, count - 1, 2)]
        return lax.ppermute(block, axes, pairs + [(j, i) for i, j in pairs])

    return swap(jnp.where(even, tail, head), 0), swap(jnp.where(even, head, tail), 1)


MEMBER, SLOT, FACE = 1, 2, 3 + FACES
CELL, TARGET = 0, FACES
LANES = 128


ROUNDS = ([(0, 2), (1, 0), (2, 3), (3, 1)], [(0, 1), (1, 3), (2, 0), (3, 2)])


def place_of(z, dest):
    if dest in (z, z ^ 3):
        return 3 if dest == z else 0
    return 1 if (z, dest) in ROUNDS[0] else 2


def call_plan(count):
    sent = [(p, 0) for p in range(count)]
    kept = [(p, 1) for p in range(count)]
    return [sent[:1], [sent[1], kept[0]], [sent[2], kept[1]], [sent[3], kept[2], kept[3]]]


def lists_kernel(elems, count, ints_ref, again_ref, code_ref, list_ref, count_ref):
    me = lax.axis_index("sub")
    z = lax.axis_index("elem")
    plan = call_plan(count)
    code = {table: (c, t) for c, tables in enumerate(plan) for t, table in enumerate(tables)}
    numbers, calls = 0, 0
    for d in range(count):
        for x in range(2):
            values = [0, 0]
            for y in range(count):
                for mine in range(2):
                    here = (z == y) & ((me == x) if mine else (me != x))
                    for i in range(2):
                        values[i] = jnp.where(here, code[place_of(y, d), mine][i], values[i])
            calls += values[0] << (2 * (2 * d + x))
            numbers += values[1] << (3 * (2 * d + x))

    device = z * lax.axis_size("sub") + me
    rim = elems // 4
    faces = again_ref[FACE:FACE + FACES, :]
    code_ref[...] = jnp.zeros_like(code_ref)
    code_ref[CELL:CELL + FACES, :elems] = jnp.where(faces >= 0, faces - (device * elems - rim), elems + 2 * rim)
    code_ref[TARGET:TARGET + FACES + 1, :elems] = (
        again_ref[MEMBER:MEMBER + 1, :] * CS + again_ref[SLOT:SLOT + FACES + 1, :])

    lengths = 0
    for start in range(0, elems, STEP):
        owners = [ints_ref[0, e] for e in range(start, start + STEP)]
        for e, owner in zip(range(start, start + STEP), owners):
            call = (calls >> (2 * owner)) & 3
            number = (numbers >> (3 * owner)) & 7
            list_ref[call, (lengths >> (8 * call)) & 127] = LANES * BLOCKS * number + (2 * LANES + e)
            lengths += 1 << (8 * call)
    for call in range(len(plan)):
        length = (lengths >> (8 * call)) & 127
        count_ref[call] = length
        for u in range(UNROLL):
            list_ref[call, length + u] = elems


def near_kernel(cells_ref, other_ref, after_ref, near_ref, weight_ref):
    near_blocks(near_ref, 0, cells_ref)
    own_weights(weight_ref, cells_ref, other_ref)


def rows_kernel(jac_ref, after_ref, rows_ref):
    width = 2048

    def step(i, carry):
        at = pl.ds(pl.multiple_of(i * STEP, STEP), STEP)
        for q in range(jac_ref.shape[1] // width):
            part = jac_ref[at, q * width:(q + 1) * width]
            rows_ref[at, q * 16:(q + 1) * 16] = pltpu.einshape("a(bc)->abc", part, b=16, c=128)
        return carry

    lax.fori_loop(0, jac_ref.shape[0] // STEP, step, 0)


def accumulate(call, elems, code_ref, list_ref, count_ref, rows_ref, near_ref, weight_ref, total):
    low = lax.broadcasted_iota(jnp.int32, (32, 128), 1) < B
    high = jnp.where(low, 0, 1)
    total[...] = jnp.zeros_like(total)

    def body(it, carry):
        items = []
        for u in range(UNROLL):
            entry = list_ref[call, it * UNROLL + u]
            at = entry & (LANES - 1)
            items.append((at, jnp.minimum(at, elems - 1), entry >> 7))
        products = []
        for at, e, base in items:
            parts = []
            for j in range(FACES + 1):
                cell = near_ref[e + elems // 4 if j == 0 else code_ref[CELL + j - 1, at]]
                zero = jnp.zeros_like(cell)
                both = jnp.concatenate([jnp.where(low, cell, zero), jnp.where(low, zero, cell)], axis=0)
                block = rows_ref[e, j * 32:(j + 1) * 32, :]
                part = lax.dot_general(both, block, NT, preferred_element_type=jnp.float32)
                parts.append(jnp.concatenate([part[:32], part[32:]], axis=1))
            products.append(jnp.concatenate(parts, axis=0).astype(jnp.bfloat16))
        results = []
        for (at, e, base), product in zip(items, products):
            own = weight_ref[e]
            own = jnp.concatenate([own, own], axis=0)
            results.append(lax.dot_general(product, own, NT, preferred_element_type=jnp.float32))
        for (at, e, base), result in zip(items, results):
            for j in range(FACES + 1):
                target = base + code_ref[TARGET + j, at]
                part = result[j * 32:(j + 1) * 32, :]
                total[target >> 1] += jnp.where(high == (target & 1), part, 0.0)
        return carry

    lax.fori_loop(0, (count_ref[call] + UNROLL - 1) // UNROLL, body, 0)


def near_blocks(near_ref, base, cells_ref):
    low = lax.broadcasted_iota(jnp.int32, (32, 128), 1) < B
    for p in range(cells_ref.shape[1] // 128):
        pair = cells_ref[:, p * 128:(p + 1) * 128].astype(jnp.float32)
        turned = pltpu.roll(pair, B, 1)
        near_ref[base + 2 * p] = jnp.where(low, pair, turned).astype(jnp.bfloat16)
        near_ref[base + 2 * p + 1] = jnp.where(low, turned, pair).astype(jnp.bfloat16)


def own_weights(weight_ref, cells_ref, other_ref):
    row = lax.broadcasted_iota(jnp.int32, (128, 128), 0)
    col = lax.broadcasted_iota(jnp.int32, (128, 128), 1)
    source = (col // B) * B + 2 * (col % 32) + (col % B) // 32
    pick = jnp.where(row == source, 1.0, 0.0).astype(jnp.bfloat16)
    low_first = lax.axis_index("col") == 0
    step = 8
    for p in range(0, cells_ref.shape[1] // 128, step):
        stacked = []
        for q in range(p, p + step):
            own, other = cells_ref[:, q * 128:(q + 1) * 128], other_ref[:, q * 128:(q + 1) * 128]
            stacked += [jnp.where(low_first, own, other), jnp.where(low_first, other, own)]
        moved = jnp.dot(jnp.concatenate(stacked, axis=0), pick, preferred_element_type=jnp.float32)
        for q in range(step):
            pair = moved[q * CB:(q + 1) * CB]
            for h in range(2):
                weight_ref[2 * (p + q) + h] = pair[:, h * B:(h + 1) * B].astype(jnp.bfloat16)


def first_kernel(elems, code_ref, list_ref, count_ref, rows_ref, own_ref, weight_ref, two_ref, one_ref, *rest):
    outs, near_ref, total = rest[:-2], rest[-2], rest[-1]
    rim = elems // 4
    device = lax.axis_index("elem") * lax.axis_size("sub") + lax.axis_index("sub")
    even = device % 2 == 0
    near_ref[rim:rim + elems] = own_ref[...]
    near_blocks(near_ref, jnp.where(even, rim + elems, 0), one_ref)
    near_blocks(near_ref, jnp.where(even, 0, rim + elems), two_ref)
    near_ref[near_ref.shape[0] - 1] = jnp.zeros((32, 128), jnp.bfloat16)
    accumulate(0, elems, code_ref, list_ref, count_ref, rows_ref, near_ref, weight_ref, total)
    for k, out in enumerate(outs):
        out[...] = total[1 + k * PAIRS // 2:1 + (k + 1) * PAIRS // 2].astype(out.dtype)


def next_kernel(elems, call, cuts, code_ref, list_ref, count_ref, rows_ref, near_ref, weight_ref, after_ref, *rest):
    outs, total = rest[:-1], rest[-1]
    accumulate(call, elems, code_ref, list_ref, count_ref, rows_ref, near_ref, weight_ref, total)
    for (t, at), out in zip(cuts, outs):
        start = 1 + t * PAIRS
        out[...] = total[start + at.start:start + at.stop].astype(out.dtype)


def add_kernel(start, joins, kept_ref, came_ref, *rest):
    out_ref = rest[-1]
    value = kept_ref[start:start + out_ref.shape[0]] + came_ref[...].astype(jnp.float32)
    if joins is not None:
        outer = (lax.axis_index("elem") + 1) % 4 < 2
        value = value + jnp.where(outer == joins, rest[0][...].astype(jnp.float32), 0.0)
    out_ref[...] = value.astype(out_ref.dtype)


def gather_kernel(own_ref, *rest):
    parts, total = rest[:-1], rest[-1]
    total[...] = own_ref[...]
    at = 0
    for part in parts:
        total[at:at + part.shape[0]] += part[...].astype(jnp.float32)
        at = (at + part.shape[0]) % PAIRS


def last_kernel(*rest):
    out_ref, total, block, done = rest[-4:]
    gather_kernel(*rest[:-4], total)
    low = lax.broadcasted_iota(jnp.int32, (32, 128), 1) < B
    copies = []
    for a in range(AGG_DEV):
        first = a * CS // 2
        for q in range(CS // 2):
            if a % 2 == 0:
                block[a, :, q * 128:(q + 1) * 128] = total[first + q]
            else:
                block[a, :, q * 128:(q + 1) * 128] = jnp.where(
                    low, pltpu.roll(total[first + q], B, 1), pltpu.roll(total[first + q + 1], B, 1))
        last = total[first + CS // 2]
        if a % 2 == 1:
            last = pltpu.roll(last, B, 1)
        block[a, :, (CS // 2) * 128:] = last[:, :B]
        if a % 2 == 1:
            pair = pl.ds(a - 1, 2)
            copies.append(pltpu.make_async_copy(block.at[pair], out_ref.at[pair], done.at[a // 2]))
            copies[-1].start()
    for copy in copies:
        copy.wait()


def dense(jacobian, prolong, face_pattern, owner, member, coarse_slot):
    elems = jacobian.shape[0]
    half = prolong.shape[0]
    count = lax.axis_size("elem")
    rim = elems // 4
    tiles = jacobian.shape[1] // 128
    plan = call_plan(count)
    cost = pl.CostEstimate(flops=1000, bytes_accessed=1000, transcendentals=0)

    other = lax.ppermute(prolong, "col", [(0, 1), (1, 0)])
    one, two = halo_swaps(prolong, rim * B)
    ints = jnp.concatenate([owner.T, member[None], coarse_slot.T, face_pattern.T], axis=0)

    long = pl.CostEstimate(flops=20_000_000_000, bytes_accessed=1000, transcendentals=0)
    codes, lists, counts = pl.pallas_call(
        functools.partial(lists_kernel, elems, count),
        in_specs=[SMEM, VMEM],
        out_specs=[VMEM, SMEM, SMEM],
        out_shape=[
            jax.ShapeDtypeStruct((16, LANES), jnp.int32),
            jax.ShapeDtypeStruct((len(plan), elems + UNROLL), jnp.int32),
            jax.ShapeDtypeStruct((len(plan),), jnp.int32),
        ],
        compiler_params=params(),
        cost_estimate=long,
        name="lists",
    )(ints, ints)
    own_near, weights = pl.pallas_call(
        near_kernel,
        in_specs=[VMEM, VMEM, pl.BlockSpec(memory_space=pl.ANY)],
        out_specs=[VMEM, VMEM],
        out_shape=[
            jax.ShapeDtypeStruct((elems, half, 2 * B), jnp.bfloat16),
            jax.ShapeDtypeStruct((elems, CB, B), jnp.bfloat16),
        ],
        compiler_params=params(),
        cost_estimate=cost,
        name="near",
    )(prolong, other, codes)
    rows = pl.pallas_call(
        rows_kernel,
        in_specs=[VMEM, pl.BlockSpec(memory_space=pl.ANY)],
        out_specs=VMEM,
        out_shape=jax.ShapeDtypeStruct((elems, tiles, 128), jnp.bfloat16),
        compiler_params=params(),
        cost_estimate=cost,
        name="rows",
    )(jacobian, own_near)

    table = (PAIRS, half, 2 * B)
    *sent, near = pl.pallas_call(
        functools.partial(first_kernel, elems),
        in_specs=[SMEM] * 3 + [VMEM] * 5,
        out_specs=[VMEM] * 3,
        out_shape=[jax.ShapeDtypeStruct((PAIRS // 2, half, 2 * B), jnp.bfloat16)] * 2 + [
            jax.ShapeDtypeStruct((elems + 2 * rim + 1, half, 2 * B), jnp.bfloat16),
        ],
        scratch_shapes=[pltpu.VMEM((1 + PAIRS, half, 2 * B), jnp.float32)],
        compiler_params=params(),
        cost_estimate=cost,
        name="first",
    )(codes, lists, counts, rows, own_near, weights, two, one)

    def across(block):
        return lax.ppermute(block, "sub", [(0, 1), (1, 0)])

    def along(block, pairs):
        return lax.ppermute(block, "elem", pairs)

    def behind(block, *others):
        return lax.optimization_barrier((block, *others))[0]

    def summed(p, at, block, joins=None, *more):
        return pl.pallas_call(
            functools.partial(add_kernel, at.start, joins),
            in_specs=[VMEM] * (2 + len(more)),
            out_specs=VMEM,
            out_shape=jax.ShapeDtypeStruct(block.shape, jnp.bfloat16),
            compiler_params=params(),
            cost_estimate=cost,
            name="add_%d" % p,
        )(kept[p], block, *more)

    whole, halves = slice(0, PAIRS), [slice(0, PAIRS // 2), slice(PAIRS // 2, PAIRS)]
    pieces = {p: halves if p < 3 else [whole] for p in range(1, count)}
    def tables(call, after):
        cuts = [(t, at) for t, (p, mine) in enumerate(plan[call]) for at in ([whole] if mine else pieces[p])]
        outs = pl.pallas_call(
            functools.partial(next_kernel, elems, call, cuts),
            in_specs=[SMEM] * 3 + [VMEM] * 3 + [pl.BlockSpec(memory_space=pl.ANY)],
            out_specs=[VMEM] * len(cuts),
            out_shape=[
                jax.ShapeDtypeStruct(
                    (at.stop - at.start, half, 2 * B), jnp.float32 if plan[call][t][1] else jnp.bfloat16)
                for t, at in cuts
            ],
            scratch_shapes=[pltpu.VMEM((1 + len(plan[call]) * PAIRS, half, 2 * B), jnp.float32)],
            compiler_params=params(),
            cost_estimate=cost,
            name="tables_%d" % call,
        )(codes, lists, counts, rows, near, weights, after)
        for (t, at), out in zip(cuts, outs):
            p, mine = plan[call][t]
            if mine:
                kept[p] = out
            else:
                ready.setdefault(p, []).append(out)

    came = {0: [across(sent[0])]}
    kept, ready = {}, {}
    tables(1, near)
    came[0].append(across(sent[1]))
    ready0 = [summed(0, halves[0], came[0][0])]
    tables(2, ready0[0])
    came[0][1] = behind(came[0][1], ready0[0])
    ready0.append(summed(0, halves[1], came[0][1]))
    joined = [along(block, [(y, y ^ 1) for y in range(count)]) for block in ready0]
    tables(3, ready0[1])
    came[1] = [across(behind(ready[1][0], came[0][0])), across(behind(ready[1][1], came[0][1]))]
    ready1 = [summed(1, at, block, True, more) for at, block, more in zip(halves, came[1], joined)]
    round1 = [along(block, ROUNDS[0]) for block in ready1]
    came[2] = [across(behind(ready[2][0], joined[0]))]
    came[2].append(across(behind(ready[2][1], came[2][0])))
    came[2][0] = behind(came[2][0], round1[0])
    came[2][1] = behind(came[2][1], round1[0], round1[1])
    ready2 = [summed(2, at, block, False, more) for at, block, more in zip(halves, came[2], joined)]
    round2 = [along(block, ROUNDS[1]) for block in ready2]
    came[3] = [across(behind(ready[3][0], came[2][0]))]

    total = pl.pallas_call(
        gather_kernel,
        in_specs=[VMEM] * 3,
        out_specs=VMEM,
        out_shape=jax.ShapeDtypeStruct(table, jnp.float32),
        compiler_params=params(),
        cost_estimate=pl.CostEstimate(flops=1_000_000_000, bytes_accessed=1000, transcendentals=0),
        name="gather",
    )(kept[count - 1], *round1)
    parts = round2 + came[count - 1]
    coarse = pl.pallas_call(
        last_kernel,
        in_specs=[VMEM] * (1 + len(parts)),
        out_specs=pl.BlockSpec(memory_space=pl.ANY),
        out_shape=jax.ShapeDtypeStruct((AGG_DEV, half, CS * CB), jnp.float32),
        scratch_shapes=[
            pltpu.VMEM(table, jnp.float32),
            pltpu.VMEM((AGG_DEV, half, CS * CB), jnp.float32),
            pltpu.SemaphoreType.DMA((AGG_DEV // 2,)),
        ],
        compiler_params=params(),
        cost_estimate=cost,
        name="last",
    )(total, *parts)
    return coarse.transpose(1, 0, 2)


def direct(jacobian, prolong, face_pattern, owner, member, coarse_slot):
    elems = jacobian.shape[0]
    owners = lax.axis_size(("elem", "sub"))
    capacity = max(2, 2 * elems // owners)
    device = lax.axis_index(("elem", "sub"))
    half = prolong.shape[0]
    rim = elems // 4
    before, after = halo(prolong, rim * B)
    ghosts = jnp.concatenate([before, prolong, after], axis=1).reshape(half, elems + 2 * rim, B)
    whole = lax.all_gather(prolong, "col", axis=0, tiled=True).reshape(CB, elems, B)
    first_row = device * elems - rim
    selfcol = jnp.arange(elems, dtype=jnp.int32)[:, None] + rim
    remote = jnp.where(face_pattern >= 0, face_pattern - first_row, 0)
    columns = jnp.concatenate([selfcol, remote], axis=1)
    present = jnp.concatenate([jnp.ones((elems, 1), jnp.bool_), face_pattern >= 0], axis=1)
    neighbour_rows = ghosts[:, columns, :] * present[None, :, :, None].astype(jnp.bfloat16)
    blocks = jacobian.reshape(elems, FACES + 1, B, B)
    product = jnp.einsum(
        "ejik,cejk->ejic", blocks, neighbour_rows, preferred_element_type=jnp.float32
    ).astype(jnp.bfloat16)
    owner_flat = owner[:, 0]
    marks = (owner_flat[:, None] == jnp.arange(owners, dtype=jnp.int32)[None, :]).astype(jnp.int32)
    ranking = jnp.sum(jnp.cumsum(marks, axis=0) * marks, axis=1) - 1
    place = owner_flat * capacity + ranking
    target = member[:, None] * CS + coarse_slot
    slots = owners * capacity
    labels = jnp.full((slots, FACES + 1), -1, jnp.int32).at[place].set(target)
    contribution = jnp.einsum("rei,ejic->ejcr", whole, product, preferred_element_type=jnp.float32)
    payload = jnp.zeros((slots, FACES + 1, half, CB), jnp.float32).at[place].set(contribution)
    axes = ("elem", "sub")
    arrived = lax.all_to_all(payload, axes, split_axis=0, concat_axis=0, tiled=True)
    arrived_labels = lax.all_to_all(labels, axes, split_axis=0, concat_axis=0, tiled=True)
    items = slots * (FACES + 1)
    values = arrived.reshape(items, half * CB)
    flat_labels = arrived_labels.reshape(items)
    destination = jnp.where(flat_labels >= 0, flat_labels, BLOCKS).astype(jnp.int32)
    summed = jnp.zeros((BLOCKS, half * CB), jnp.float32).at[destination].add(values, mode="drop")
    summed = summed.reshape(AGG_DEV, CS, half, CB).transpose(2, 0, 1, 3)
    return summed.reshape(half, AGG_DEV, CS * CB)


def shards(jacobian, *rest):
    elems = jacobian.shape[0]
    owners = lax.axis_size(("elem", "sub"))
    capacity = max(2, 2 * elems // owners)
    if lax.axis_size("sub") == 2 and lax.axis_size("elem") == 4 and BLOCKS <= capacity * (FACES + 1):
        return dense(jacobian, *rest)
    return direct(jacobian, *rest)


def solution(mesh):
    in_specs = (
        P(("groups", "elem", "sub"), None),
        P("col", ("groups", "elem", "sub")),
        P(("groups", "elem", "sub"), None),
        P(("groups", "elem", "sub"), None),
        P(("groups", "elem", "sub")),
        P(("groups", "elem", "sub"), None),
    )
    out_specs = P("col", ("groups", "elem", "sub"), None)
    return jax.shard_map(shards, mesh=mesh, in_specs=in_specs, out_specs=out_specs, check_vma=False)
```

```python
import functools

import jax
import jax.numpy as jnp
from jax import lax
from jax.experimental import pallas as pl
from jax.experimental.pallas import tpu as pltpu
from jax.sharding import PartitionSpec as P

B = 64
CB = 64
FACES = 4
CS = 9
AGG_DEV = 12
BLOCKS = AGG_DEV * CS
PAIRS = BLOCKS // 2
STEP = 16
UNROLL = 8
VMEM = pl.BlockSpec(memory_space=pltpu.VMEM)
SMEM = pl.BlockSpec(memory_space=pltpu.SMEM)
NT = (((1,), (1,)), ((), ()))


def params(mib=16):
    return pltpu.CompilerParams(vmem_limit_bytes=mib * 1024 * 1024)


def halo(cells, width):
    axes = ("elem", "sub")
    count = lax.axis_size(axes)
    up = [(i, i + 1) for i in range(count - 1)]
    down = [(i + 1, i) for i in range(count - 1)]
    return (
        lax.ppermute(cells[:, -width:], axes, up),
        lax.ppermute(cells[:, :width], axes, down),
    )


def halo_swaps(cells, width):
    axes = ("elem", "sub")
    count = lax.axis_size(axes)
    even = lax.axis_index(axes) % 2 == 0
    tail, head = cells[:, -width:], cells[:, :width]

    def swap(block, first):
        pairs = [(i, i + 1) for i in range(first, count - 1, 2)]
        return lax.ppermute(block, axes, pairs + [(j, i) for i, j in pairs])

    return swap(jnp.where(even, tail, head), 0), swap(jnp.where(even, head, tail), 1)


MEMBER, SLOT, FACE = 1, 2, 3 + FACES
CELL, TARGET = 0, FACES
LANES = 128


ROUNDS = ([(0, 2), (1, 0), (2, 3), (3, 1)], [(0, 1), (1, 3), (2, 0), (3, 2)])


def place_of(z, dest):
    if dest in (z, z ^ 3):
        return 3 if dest == z else 0
    return 1 if (z, dest) in ROUNDS[0] else 2


def call_plan(count):
    sent = [(p, 0) for p in range(count)]
    kept = [(p, 1) for p in range(count)]
    return [sent[:1], [sent[1], kept[0]], [sent[2], kept[1]], [sent[3], kept[2], kept[3]]]


def lists_kernel(elems, count, ints_ref, again_ref, code_ref, list_ref, count_ref):
    me = lax.axis_index("sub")
    z = lax.axis_index("elem")
    plan = call_plan(count)
    code = {table: (c, t) for c, tables in enumerate(plan) for t, table in enumerate(tables)}
    numbers, calls = 0, 0
    for d in range(count):
        for x in range(2):
            values = [0, 0]
            for y in range(count):
                for mine in range(2):
                    here = (z == y) & ((me == x) if mine else (me != x))
                    for i in range(2):
                        values[i] = jnp.where(here, code[place_of(y, d), mine][i], values[i])
            calls += values[0] << (2 * (2 * d + x))
            numbers += values[1] << (3 * (2 * d + x))

    device = z * lax.axis_size("sub") + me
    rim = elems // 4
    faces = again_ref[FACE:FACE + FACES, :]
    code_ref[...] = jnp.zeros_like(code_ref)
    code_ref[CELL:CELL + FACES, :elems] = jnp.where(faces >= 0, faces - (device * elems - rim), elems + 2 * rim)
    code_ref[TARGET:TARGET + FACES + 1, :elems] = (
        again_ref[MEMBER:MEMBER + 1, :] * CS + again_ref[SLOT:SLOT + FACES + 1, :])

    lengths = 0
    for start in range(0, elems, STEP):
        owners = [ints_ref[0, e] for e in range(start, start + STEP)]
        for e, owner in zip(range(start, start + STEP), owners):
            call = (calls >> (2 * owner)) & 3
            number = (numbers >> (3 * owner)) & 7
            list_ref[call, (lengths >> (8 * call)) & 127] = LANES * BLOCKS * number + (2 * LANES + e)
            lengths += 1 << (8 * call)
    for call in range(len(plan)):
        length = (lengths >> (8 * call)) & 127
        count_ref[call] = length
        for u in range(UNROLL):
            list_ref[call, length + u] = elems


def near_kernel(cells_ref, other_ref, after_ref, near_ref, weight_ref):
    near_blocks(near_ref, 0, cells_ref)
    own_weights(weight_ref, cells_ref, other_ref)


def rows_kernel(jac_ref, after_ref, rows_ref):
    width = 2048

    def step(i, carry):
        at = pl.ds(pl.multiple_of(i * STEP, STEP), STEP)
        for q in range(jac_ref.shape[1] // width):
            part = jac_ref[at, q * width:(q + 1) * width]
            rows_ref[at, q * 16:(q + 1) * 16] = pltpu.einshape("a(bc)->abc", part, b=16, c=128)
        return carry

    lax.fori_loop(0, jac_ref.shape[0] // STEP, step, 0)


def accumulate(call, elems, code_ref, list_ref, count_ref, rows_ref, near_ref, weight_ref, total):
    low = lax.broadcasted_iota(jnp.int32, (32, 128), 1) < B
    high = jnp.where(low, 0, 1)
    total[...] = jnp.zeros_like(total)

    def body(it, carry):
        items = []
        for u in range(UNROLL):
            entry = list_ref[call, it * UNROLL + u]
            at = entry & (LANES - 1)
            items.append((at, jnp.minimum(at, elems - 1), entry >> 7))
        products = []
        for at, e, base in items:
            parts = []
            for j in range(FACES + 1):
                cell = near_ref[e + elems // 4 if j == 0 else code_ref[CELL + j - 1, at]]
                zero = jnp.zeros_like(cell)
                both = jnp.concatenate([jnp.where(low, cell, zero), jnp.where(low, zero, cell)], axis=0)
                block = rows_ref[e, j * 32:(j + 1) * 32, :]
                part = lax.dot_general(both, block, NT, preferred_element_type=jnp.float32)
                parts.append(jnp.concatenate([part[:32], part[32:]], axis=1))
            products.append(jnp.concatenate(parts, axis=0).astype(jnp.bfloat16))
        results = []
        for (at, e, base), product in zip(items, products):
            own = weight_ref[e]
            own = jnp.concatenate([own, own], axis=0)
            results.append(lax.dot_general(product, own, NT, preferred_element_type=jnp.float32))
        for (at, e, base), result in zip(items, results):
            for j in range(FACES + 1):
                target = base + code_ref[TARGET + j, at]
                part = result[j * 32:(j + 1) * 32, :]
                total[target >> 1] += jnp.where(high == (target & 1), part, 0.0)
        return carry

    lax.fori_loop(0, (count_ref[call] + UNROLL - 1) // UNROLL, body, 0)


def near_blocks(near_ref, base, cells_ref):
    low = lax.broadcasted_iota(jnp.int32, (32, 128), 1) < B
    for p in range(cells_ref.shape[1] // 128):
        pair = cells_ref[:, p * 128:(p + 1) * 128].astype(jnp.float32)
        turned = pltpu.roll(pair, B, 1)
        near_ref[base + 2 * p] = jnp.where(low, pair, turned).astype(jnp.bfloat16)
        near_ref[base + 2 * p + 1] = jnp.where(low, turned, pair).astype(jnp.bfloat16)


def own_weights(weight_ref, cells_ref, other_ref):
    row = lax.broadcasted_iota(jnp.int32, (128, 128), 0)
    col = lax.broadcasted_iota(jnp.int32, (128, 128), 1)
    source = (col // B) * B + 2 * (col % 32) + (col % B) // 32
    pick = jnp.where(row == source, 1.0, 0.0).astype(jnp.bfloat16)
    low_first = lax.axis_index("col") == 0
    step = 8
    for p in range(0, cells_ref.shape[1] // 128, step):
        stacked = []
        for q in range(p, p + step):
            own, other = cells_ref[:, q * 128:(q + 1) * 128], other_ref[:, q * 128:(q + 1) * 128]
            stacked += [jnp.where(low_first, own, other), jnp.where(low_first, other, own)]
        moved = jnp.dot(jnp.concatenate(stacked, axis=0), pick, preferred_element_type=jnp.float32)
        for q in range(step):
            pair = moved[q * CB:(q + 1) * CB]
            for h in range(2):
                weight_ref[2 * (p + q) + h] = pair[:, h * B:(h + 1) * B].astype(jnp.bfloat16)


def first_kernel(elems, code_ref, list_ref, count_ref, rows_ref, own_ref, weight_ref, two_ref, one_ref, *rest):
    outs, near_ref, total = rest[:-2], rest[-2], rest[-1]
    rim = elems // 4
    device = lax.axis_index("elem") * lax.axis_size("sub") + lax.axis_index("sub")
    even = device % 2 == 0
    near_ref[rim:rim + elems] = own_ref[...]
    near_blocks(near_ref, jnp.where(even, rim + elems, 0), one_ref)
    near_blocks(near_ref, jnp.where(even, 0, rim + elems), two_ref)
    near_ref[near_ref.shape[0] - 1] = jnp.zeros((32, 128), jnp.bfloat16)
    accumulate(0, elems, code_ref, list_ref, count_ref, rows_ref, near_ref, weight_ref, total)
    for k, out in enumerate(outs):
        out[...] = total[1 + k * PAIRS // 2:1 + (k + 1) * PAIRS // 2].astype(out.dtype)


def next_kernel(elems, call, cuts, code_ref, list_ref, count_ref, rows_ref, near_ref, weight_ref, after_ref, *rest):
    outs, total = rest[:-1], rest[-1]
    accumulate(call, elems, code_ref, list_ref, count_ref, rows_ref, near_ref, weight_ref, total)
    for (t, at), out in zip(cuts, outs):
        start = 1 + t * PAIRS
        out[...] = total[start + at.start:start + at.stop].astype(out.dtype)


def add_kernel(start, joins, kept_ref, came_ref, *rest):
    out_ref = rest[-1]
    value = kept_ref[start:start + out_ref.shape[0]] + came_ref[...].astype(jnp.float32)
    if joins is not None:
        outer = (lax.axis_index("elem") + 1) % 4 < 2
        value = value + jnp.where(outer == joins, rest[0][...].astype(jnp.float32), 0.0)
    out_ref[...] = value.astype(out_ref.dtype)


def gather_kernel(own_ref, *rest):
    parts, total = rest[:-1], rest[-1]
    total[...] = own_ref[...]
    at = 0
    for part in parts:
        total[at:at + part.shape[0]] += part[...].astype(jnp.float32)
        at = (at + part.shape[0]) % PAIRS


def last_kernel(*rest):
    out_ref, total, block, done = rest[-4:]
    gather_kernel(*rest[:-4], total)
    low = lax.broadcasted_iota(jnp.int32, (32, 128), 1) < B
    copies = []
    for a in range(AGG_DEV):
        first = a * CS // 2
        for q in range(CS // 2):
            if a % 2 == 0:
                block[a, :, q * 128:(q + 1) * 128] = total[first + q]
            else:
                block[a, :, q * 128:(q + 1) * 128] = jnp.where(
                    low, pltpu.roll(total[first + q], B, 1), pltpu.roll(total[first + q + 1], B, 1))
        last = total[first + CS // 2]
        if a % 2 == 1:
            last = pltpu.roll(last, B, 1)
        block[a, :, (CS // 2) * 128:] = last[:, :B]
        if a % 2 == 1:
            pair = pl.ds(a - 1, 2)
            copies.append(pltpu.make_async_copy(block.at[pair], out_ref.at[pair], done.at[a // 2]))
            copies[-1].start()
    for copy in copies:
        copy.wait()


def dense(jacobian, prolong, face_pattern, owner, member, coarse_slot):
    elems = jacobian.shape[0]
    half = prolong.shape[0]
    count = lax.axis_size("elem")
    rim = elems // 4
    tiles = jacobian.shape[1] // 128
    plan = call_plan(count)
    cost = pl.CostEstimate(flops=1000, bytes_accessed=1000, transcendentals=0)

    other = lax.ppermute(prolong, "col", [(0, 1), (1, 0)])
    one, two = halo_swaps(prolong, rim * B)
    ints = jnp.concatenate([owner.T, member[None], coarse_slot.T, face_pattern.T], axis=0)

    long = pl.CostEstimate(flops=20_000_000_000, bytes_accessed=1000, transcendentals=0)
    codes, lists, counts = pl.pallas_call(
        functools.partial(lists_kernel, elems, count),
        in_specs=[SMEM, VMEM],
        out_specs=[VMEM, SMEM, SMEM],
        out_shape=[
            jax.ShapeDtypeStruct((16, LANES), jnp.int32),
            jax.ShapeDtypeStruct((len(plan), elems + UNROLL), jnp.int32),
            jax.ShapeDtypeStruct((len(plan),), jnp.int32),
        ],
        compiler_params=params(),
        cost_estimate=long,
        name="lists",
    )(ints, ints)
    own_near, weights = pl.pallas_call(
        near_kernel,
        in_specs=[VMEM, VMEM, pl.BlockSpec(memory_space=pl.ANY)],
        out_specs=[VMEM, VMEM],
        out_shape=[
            jax.ShapeDtypeStruct((elems, half, 2 * B), jnp.bfloat16),
            jax.ShapeDtypeStruct((elems, CB, B), jnp.bfloat16),
        ],
        compiler_params=params(),
        cost_estimate=cost,
        name="near",
    )(prolong, other, codes)
    rows = pl.pallas_call(
        rows_kernel,
        in_specs=[VMEM, pl.BlockSpec(memory_space=pl.ANY)],
        out_specs=VMEM,
        out_shape=jax.ShapeDtypeStruct((elems, tiles, 128), jnp.bfloat16),
        compiler_params=params(),
        cost_estimate=cost,
        name="rows",
    )(jacobian, own_near)

    table = (PAIRS, half, 2 * B)
    *sent, near = pl.pallas_call(
        functools.partial(first_kernel, elems),
        in_specs=[SMEM] * 3 + [VMEM] * 5,
        out_specs=[VMEM] * 3,
        out_shape=[jax.ShapeDtypeStruct((PAIRS // 2, half, 2 * B), jnp.bfloat16)] * 2 + [
            jax.ShapeDtypeStruct((elems + 2 * rim + 1, half, 2 * B), jnp.bfloat16),
        ],
        scratch_shapes=[pltpu.VMEM((1 + PAIRS, half, 2 * B), jnp.float32)],
        compiler_params=params(),
        cost_estimate=cost,
        name="first",
    )(codes, lists, counts, rows, own_near, weights, two, one)

    def across(block):
        return lax.ppermute(block, "sub", [(0, 1), (1, 0)])

    def along(block, pairs):
        return lax.ppermute(block, "elem", pairs)

    def behind(block, *others):
        return lax.optimization_barrier((block, *others))[0]

    def summed(p, at, block, joins=None, *more):
        return pl.pallas_call(
            functools.partial(add_kernel, at.start, joins),
            in_specs=[VMEM] * (2 + len(more)),
            out_specs=VMEM,
            out_shape=jax.ShapeDtypeStruct(block.shape, jnp.bfloat16),
            compiler_params=params(),
            cost_estimate=cost,
            name="add_%d" % p,
        )(kept[p], block, *more)

    whole, halves = slice(0, PAIRS), [slice(0, PAIRS // 2), slice(PAIRS // 2, PAIRS)]
    pieces = {p: halves if p < 3 else [whole] for p in range(1, count)}
    def tables(call, after):
        cuts = [(t, at) for t, (p, mine) in enumerate(plan[call]) for at in ([whole] if mine else pieces[p])]
        outs = pl.pallas_call(
            functools.partial(next_kernel, elems, call, cuts),
            in_specs=[SMEM] * 3 + [VMEM] * 3 + [pl.BlockSpec(memory_space=pl.ANY)],
            out_specs=[VMEM] * len(cuts),
            out_shape=[
                jax.ShapeDtypeStruct(
                    (at.stop - at.start, half, 2 * B), jnp.float32 if plan[call][t][1] else jnp.bfloat16)
                for t, at in cuts
            ],
            scratch_shapes=[pltpu.VMEM((1 + len(plan[call]) * PAIRS, half, 2 * B), jnp.float32)],
            compiler_params=params(),
            cost_estimate=cost,
            name="tables_%d" % call,
        )(codes, lists, counts, rows, near, weights, after)
        for (t, at), out in zip(cuts, outs):
            p, mine = plan[call][t]
            if mine:
                kept[p] = out
            else:
                ready.setdefault(p, []).append(out)

    came = {0: [across(sent[0])]}
    kept, ready = {}, {}
    tables(1, near)
    came[0].append(across(sent[1]))
    ready0 = [summed(0, halves[0], came[0][0])]
    tables(2, ready0[0])
    came[0][1] = behind(came[0][1], ready[2][0])
    ready0.append(summed(0, halves[1], came[0][1]))
    joined = [along(block, [(y, y ^ 1) for y in range(count)]) for block in ready0]
    tables(3, ready0[1])
    came[1] = [across(behind(ready[1][0], came[0][0])), across(behind(ready[1][1], came[0][1]))]
    ready1 = [summed(1, at, block, True, more) for at, block, more in zip(halves, came[1], joined)]
    round1 = [along(block, ROUNDS[0]) for block in ready1]
    came[2] = [across(behind(ready[2][0], joined[0]))]
    came[2].append(across(behind(ready[2][1], came[2][0])))
    came[2][0] = behind(came[2][0], round1[0])
    came[2][1] = behind(came[2][1], round1[0], round1[1])
    ready2 = [summed(2, at, block, False, more) for at, block, more in zip(halves, came[2], joined)]
    round2 = [along(block, ROUNDS[1]) for block in ready2]
    came[3] = [across(behind(ready[3][0], came[2][0]))]

    total = pl.pallas_call(
        gather_kernel,
        in_specs=[VMEM] * 3,
        out_specs=VMEM,
        out_shape=jax.ShapeDtypeStruct(table, jnp.float32),
        compiler_params=params(),
        cost_estimate=pl.CostEstimate(flops=1_000_000_000, bytes_accessed=1000, transcendentals=0),
        name="gather",
    )(kept[count - 1], *round1)
    parts = round2 + came[count - 1]
    coarse = pl.pallas_call(
        last_kernel,
        in_specs=[VMEM] * (1 + len(parts)),
        out_specs=pl.BlockSpec(memory_space=pl.ANY),
        out_shape=jax.ShapeDtypeStruct((AGG_DEV, half, CS * CB), jnp.float32),
        scratch_shapes=[
            pltpu.VMEM(table, jnp.float32),
            pltpu.VMEM((AGG_DEV, half, CS * CB), jnp.float32),
            pltpu.SemaphoreType.DMA((AGG_DEV // 2,)),
        ],
        compiler_params=params(),
        cost_estimate=cost,
        name="last",
    )(total, *parts)
    return coarse.transpose(1, 0, 2)


def direct(jacobian, prolong, face_pattern, owner, member, coarse_slot):
    elems = jacobian.shape[0]
    owners = lax.axis_size(("elem", "sub"))
    capacity = max(2, 2 * elems // owners)
    device = lax.axis_index(("elem", "sub"))
    half = prolong.shape[0]
    rim = elems // 4
    before, after = halo(prolong, rim * B)
    ghosts = jnp.concatenate([before, prolong, after], axis=1).reshape(half, elems + 2 * rim, B)
    whole = lax.all_gather(prolong, "col", axis=0, tiled=True).reshape(CB, elems, B)
    first_row = device * elems - rim
    selfcol = jnp.arange(elems, dtype=jnp.int32)[:, None] + rim
    remote = jnp.where(face_pattern >= 0, face_pattern - first_row, 0)
    columns = jnp.concatenate([selfcol, remote], axis=1)
    present = jnp.concatenate([jnp.ones((elems, 1), jnp.bool_), face_pattern >= 0], axis=1)
    neighbour_rows = ghosts[:, columns, :] * present[None, :, :, None].astype(jnp.bfloat16)
    blocks = jacobian.reshape(elems, FACES + 1, B, B)
    product = jnp.einsum(
        "ejik,cejk->ejic", blocks, neighbour_rows, preferred_element_type=jnp.float32
    ).astype(jnp.bfloat16)
    owner_flat = owner[:, 0]
    marks = (owner_flat[:, None] == jnp.arange(owners, dtype=jnp.int32)[None, :]).astype(jnp.int32)
    ranking = jnp.sum(jnp.cumsum(marks, axis=0) * marks, axis=1) - 1
    place = owner_flat * capacity + ranking
    target = member[:, None] * CS + coarse_slot
    slots = owners * capacity
    labels = jnp.full((slots, FACES + 1), -1, jnp.int32).at[place].set(target)
    contribution = jnp.einsum("rei,ejic->ejcr", whole, product, preferred_element_type=jnp.float32)
    payload = jnp.zeros((slots, FACES + 1, half, CB), jnp.float32).at[place].set(contribution)
    axes = ("elem", "sub")
    arrived = lax.all_to_all(payload, axes, split_axis=0, concat_axis=0, tiled=True)
    arrived_labels = lax.all_to_all(labels, axes, split_axis=0, concat_axis=0, tiled=True)
    items = slots * (FACES + 1)
    values = arrived.reshape(items, half * CB)
    flat_labels = arrived_labels.reshape(items)
    destination = jnp.where(flat_labels >= 0, flat_labels, BLOCKS).astype(jnp.int32)
    summed = jnp.zeros((BLOCKS, half * CB), jnp.float32).at[destination].add(values, mode="drop")
    summed = summed.reshape(AGG_DEV, CS, half, CB).transpose(2, 0, 1, 3)
    return summed.reshape(half, AGG_DEV, CS * CB)


def shards(jacobian, *rest):
    elems = jacobian.shape[0]
    owners = lax.axis_size(("elem", "sub"))
    capacity = max(2, 2 * elems // owners)
    if lax.axis_size("sub") == 2 and lax.axis_size("elem") == 4 and BLOCKS <= capacity * (FACES + 1):
        return dense(jacobian, *rest)
    return direct(jacobian, *rest)


def solution(mesh):
    in_specs = (
        P(("groups", "elem", "sub"), None),
        P("col", ("groups", "elem", "sub")),
        P(("groups", "elem", "sub"), None),
        P(("groups", "elem", "sub"), None),
        P(("groups", "elem", "sub")),
        P(("groups", "elem", "sub"), None),
    )
    out_specs = P("col", ("groups", "elem", "sub"), None)
    return jax.shard_map(shards, mesh=mesh, in_specs=in_specs, out_specs=out_specs, check_vma=False)
```
